512 devices in a mesh: tm: 64 (over x, z), col: 8 (over y, core).
Axes of the slice: x: 4, y: 4, z: 16, core: 2. Of those that a mesh axis runs over, the one named last changes fastest.
Arguments:
- observations: bfloat16 [8192, 8192], P(('tm', 'col')), may hold values from -6 to 6
- site_start: int32 [8192], P(('tm', 'col')), may hold values from 0 to 4095
- site_count: int32 [8192], P(('tm', 'col')), may hold values from 2048 to 8192
- site_gain: bfloat16 [8192, 1024], P(('tm', 'col')), may hold values from -0.0625 to 0.0625
- site_loading: bfloat16 [8192, 1024], P(('tm', 'col')), may hold values from -0.1875 to 0.1875
- decay: float32 [8192, 1024], P('tm'), may hold values from 0 to 1, as said below
- persistence: float32 [1024], replicated, may hold values from 0 to 1, as said below
Outputs:
- smoothed: float32 [8192, 1024], P('tm', 'col')
- predicted: bfloat16 [8192, 8192], P(('tm', 'col'))
The draws below stay inside these ranges and needn't reach their ends.
Inputs may be any that keep to these rules, and one draw needn't show every extreme that they name: Station s reports from step site_start[s] for site_count[s] steps, cut at the last step. Every decay lies strictly between 0 and 1. `persistence`: every factor lies strictly between 0 and 1.
All inputs are finite; a program needn't handle non-finite values.
Results may differ from the reference program's by a relative error of at most 0.0049.
Values may be sent and summed in bfloat16 or wider, within the bound.
No kernel may reach another device: no remote copies, remote signals or barrier semaphores. Data moves between devices by JAX's collectives and lax.ppermute only.
A program may use at most 64 MiB of HBM per device.

```python
import jax
import jax.numpy as jnp
from jax import lax

S = 1024
EPOCH_COUNT_ALL = 8192
NSITES = 8192


def slow_set(key, chance):
    return jax.random.uniform(key, (S,)) < chance


def draw_decay(key, part):
    chance = 0.5
    slow = slow_set(key, chance)
    key = jax.random.fold_in(key, 11)
    sampler_seeds = jax.random.split(key, 5)
    fast_rate = 1.0 / jax.random.uniform(sampler_seeds[0], (S,), jnp.float32, 30.0, 50.0)
    gradual_speed = jax.random.uniform(sampler_seeds[1], (S,), jnp.float32, 0.2, 0.8) / EPOCH_COUNT_ALL
    base_rate = jnp.where(slow, gradual_speed, fast_rate)
    jitter = jax.random.uniform(sampler_seeds[2], (EPOCH_COUNT_ALL, S), jnp.float32, 0.5, 1.5)
    shock_pulses = jax.random.randint(sampler_seeds[3], (2,), 0, EPOCH_COUNT_ALL)
    epoch_position = jnp.arange(EPOCH_COUNT_ALL)[:, None]
    hit_indicator = (epoch_position == shock_pulses[0]) | (epoch_position == shock_pulses[1])
    factor = jax.random.uniform(sampler_seeds[4], (EPOCH_COUNT_ALL, S), jnp.float32, 0.6, 0.85)
    return jnp.exp(-base_rate[None, :] * jitter) * jnp.where(hit_indicator, factor, 1.0)


def draw_persistence(key, part):
    chance = 0.5
    slow = slow_set(key, chance)
    key = jax.random.fold_in(key, 12)
    sampler_seeds = jax.random.split(key, 2)
    fast_rate = 1.0 / jax.random.uniform(sampler_seeds[0], (S,), jnp.float32, 30.0, 50.0)
    gradual_speed = jax.random.uniform(sampler_seeds[1], (S,), jnp.float32, 0.2, 0.8) / EPOCH_COUNT_ALL
    return jnp.exp(-jnp.where(slow, gradual_speed, fast_rate))


def plant(array, own_key, smallest, high):
    spot = [jax.random.randint(jax.random.fold_in(own_key, axis), (), 0, length) for axis, length in enumerate(array.shape)]
    widest = array.shape.index(max(array.shape))
    next_to = spot[:widest] + [(spot[widest] + 1) % array.shape[widest]] + spot[widest + 1:]
    return array.at[tuple(spot)].set(smallest).at[tuple(next_to)].set(high)


def block_levels(rng, dims, cuts, least, high):
    loudness, own = 1.0, jax.random.fold_in(rng, 6)
    for axis_at, parts in cuts:
        steps = jnp.exp(jax.random.uniform(jax.random.fold_in(own, axis_at), (parts,), jnp.float32, least / len(cuts), high / len(cuts)))
        loudness = loudness * jnp.repeat(steps, dims[axis_at] // parts).reshape([-1 if axis == axis_at else 1 for axis in range(len(dims))])
    return loudness


def normal_values(key, shape, scale, most, shards=(), held_as=jnp.bfloat16):
    values = jax.random.normal(key, shape, jnp.float32) * scale
    if len(shards) > 0:
        values = block_levels(key, shape, shards, -0.22, 0.18) * values
    return jnp.clip(values, min=-most, max=most).astype(held_as)


def setup_inputs(seed: int = 0) -> dict:
    key_of = jax.random.split(jax.random.key(seed), 8)
    observations = normal_values(key_of[0], (NSITES, EPOCH_COUNT_ALL), 1.0, 6.0, ((0, 512),))
    site_start = plant(jax.random.randint(key_of[1], (NSITES,), 0, EPOCH_COUNT_ALL // 2), jax.random.fold_in(key_of[1], 1), 0, (EPOCH_COUNT_ALL // 2) - 1).astype(jnp.int32)
    site_count = plant(jax.random.randint(key_of[2], (NSITES,), EPOCH_COUNT_ALL // 4, EPOCH_COUNT_ALL + 1), jax.random.fold_in(key_of[2], 1), EPOCH_COUNT_ALL // 4, EPOCH_COUNT_ALL).astype(jnp.int32)
    site_gain = normal_values(key_of[3], (NSITES, S), NSITES ** -0.5, 0.0625, ((0, 512),))
    site_loading = normal_values(key_of[4], (NSITES, S), S ** -0.5, 0.1875, ((0, 512),))
    decay = draw_decay(jax.random.fold_in(key_of[7], 71), 0)
    persistence = draw_persistence(jax.random.fold_in(key_of[7], 71), 0)
    return dict(observations=observations, site_start=site_start, site_count=site_count, site_gain=site_gain, site_loading=site_loading, decay=decay, persistence=persistence)


def combine(earlier, later_half):
    return (later_half[0] * earlier[0], later_half[0] * earlier[1] + later_half[1])

def reference(observations, site_start, site_count, site_gain, site_loading, decay, persistence):
    epoch_position = lax.broadcasted_iota(jnp.int32, observations.shape, 1)
    start_col = site_start[:, None]
    reporting = (epoch_position >= start_col) & (epoch_position < start_col + site_count[:, None])
    masked = jnp.where(reporting, observations, jnp.zeros_like(observations))
    driving = lax.dot_general(masked, site_gain, (((0,), (0,)), ((), ())), preferred_element_type=jnp.float32)
    inject = jnp.sqrt(1.0 - decay * decay) * driving
    decayed, filtered = lax.associative_scan(combine, (decay, inject), axis=0)
    carry_rate = persistence[None, :] * decay
    weight = (1.0 - carry_rate * decay) * filtered
    products, smoothed = lax.associative_scan(combine, (carry_rate, weight), reverse=True, axis=0)
    rounded = smoothed.astype(jnp.bfloat16)
    predicted = lax.dot_general(site_loading, rounded, (((1,), (1,)), ((), ())), preferred_element_type=jnp.float32)
    return (smoothed, predicted.astype(jnp.bfloat16))
```

```python
import jax
import jax.numpy as jnp
from jax import lax
from jax.experimental import pallas as pl
from jax.experimental.pallas import tpu as pltpu
from jax.sharding import Mesh, PartitionSpec as P

ROWS = 8
STEPS = 4


def front_kernel(start_ref, count_ref, values_ref, gain_ref, out_ref):
    devices, sites, width = out_ref.shape
    span = width - gain_ref.shape[1]
    first = pl.program_id(0) * devices
    site = lax.broadcasted_iota(jnp.int32, (sites, span), 0)
    start = end = jnp.zeros((sites, span), jnp.int32)
    for s in range(sites):
        start = jnp.where(site == s, start_ref[s], start)
        end = jnp.where(site == s, start_ref[s] + count_ref[s], end)
    epoch = lax.broadcasted_iota(jnp.int32, (sites, span), 1) + first * span
    for to in range(devices):
        values = values_ref[:, to * span:(to + 1) * span].astype(jnp.float32)
        inside = (epoch + to * span >= start) & (epoch + to * span < end)
        out_ref[to, :, :span] = jnp.where(inside, values, 0.0).astype(out_ref.dtype)
        out_ref[to, :, span:] = gain_ref[...]


def drive_kernel(got_ref, out_ref):
    sources, sites, _ = got_ref.shape
    blocks, parts, slab, share = out_ref.shape
    span = parts * slab
    rows = got_ref[:, :, :span].reshape(sources * sites, span)
    gains = got_ref[:, :, span:].reshape(sources * sites, blocks * share)
    partial = lax.dot_general(rows, gains, (((0,), (0,)), ((), ())), preferred_element_type=jnp.float32)
    partial = partial.astype(out_ref.dtype)
    for block in range(blocks):
        for part in range(parts):
            out_ref[block, part] = partial[part * slab:(part + 1) * slab, block * share:(block + 1) * share]


def shifted(value, by, fill):
    count = value.shape[0]
    row = lax.broadcasted_iota(jnp.int32, value.shape, 0)
    moved = pltpu.roll(value, by % count, 0)
    inside = row >= by if by > 0 else row < count + by
    return jnp.where(inside, moved, fill)


def across(rate, states, sign):
    step = 1
    while step < ROWS:
        states = [s + rate * shifted(s, sign * step, 0.0) for s in states]
        rate = rate * shifted(rate, sign * step, 1.0)
        step *= 2
    return shifted(rate, sign, 1.0), [shifted(s, sign, 0.0) for s in states]


def scan_kernel(parts_ref, decay_ref, persist_ref, smooth_ref, entry_ref, product_ref, summary_ref, inj):
    sources, slab, width = parts_ref.shape
    total = parts_ref[0].astype(jnp.float32)
    for source in range(1, sources):
        total = total + parts_ref[source].astype(jnp.float32)
    inj[...] = jnp.sqrt(1.0 - decay_ref[...] * decay_ref[...]) * total
    depth = slab // ROWS
    persist = persist_ref[...]

    def rows(ref, j):
        return ref[pl.ds(j, ROWS, stride=depth), :]

    decays = [rows(decay_ref, j) for j in range(depth)]
    decayed, local = [decays[0]], [rows(inj, 0)]
    for j in range(1, depth):
        decayed.append(decays[j] * decayed[-1])
        local.append(decays[j] * local[-1] + rows(inj, j))
    enter_rate, (enter,) = across(decayed[-1], [local[-1]], 1)
    local = [h + a * enter for h, a in zip(local, decayed)]
    decayed = [a * enter_rate for a in decayed]
    products, smooth, entry = [None] * depth, [None] * depth, [None] * depth
    for j in reversed(range(depth)):
        rate = persist * decays[j]
        keep = 1.0 - rate * decays[j]
        if j == depth - 1:
            products[j], smooth[j], entry[j] = rate, keep * local[j], keep * decayed[j]
        else:
            products[j] = rate * products[j + 1]
            smooth[j] = rate * smooth[j + 1] + keep * local[j]
            entry[j] = rate * entry[j + 1] + keep * decayed[j]
    leave_rate, (leave_smooth, leave_entry) = across(products[0], [smooth[0], entry[0]], -1)
    for j in range(depth):
        smooth[j] = smooth[j] + products[j] * leave_smooth
        entry[j] = entry[j] + products[j] * leave_entry
        products[j] = products[j] * leave_rate
        smooth_ref[pl.ds(j, ROWS, stride=depth), :] = smooth[j]
        entry_ref[pl.ds(j, ROWS, stride=depth), :] = entry[j]
        product_ref[pl.ds(j, ROWS, stride=depth), :] = products[j]
    summary = [decayed[-1][ROWS - 1:], local[-1][ROWS - 1:], products[0][:1], smooth[0][:1], entry[0][:1]]
    summary = jnp.concatenate(summary + [jnp.zeros((3, width), jnp.float32)], axis=0)
    for to in range(summary_ref.shape[0]):
        summary_ref[to] = summary


def finish_kernel(place_ref, slabs_ref, smooth_ref, entry_ref, product_ref, out_ref, rounded_ref, fwd, bwd):
    count, _, width = slabs_ref.shape

    def of(at, what):
        return slabs_ref[at, what:what + 1, :]

    state = jnp.zeros((1, width), jnp.float32)
    for at in range(count):
        fwd[at:at + 1, :] = state
        state = of(at, 0) * state + of(at, 1)
    state = jnp.zeros((1, width), jnp.float32)
    for at in reversed(range(count)):
        bwd[at:at + 1, :] = state
        state = of(at, 2) * state + (of(at, 3) + of(at, 4) * fwd[at:at + 1, :])
    place = place_ref[0]
    f_in, g_in = fwd[pl.ds(place, 1), :], bwd[pl.ds(place, 1), :]
    smoothed = smooth_ref[...] + entry_ref[...] * f_in + product_ref[...] * g_in
    out_ref[...] = smoothed
    rounded_ref[...] = smoothed.T.astype(rounded_ref.dtype)


def predict_kernel(loading_ref, rounded_ref, out_ref):
    blocks, parts, share, slab = rounded_ref.shape
    devices, sites, _ = out_ref.shape
    loadings = loading_ref[...]
    for part in range(parts):
        states = rounded_ref[:, part].reshape(blocks * share, slab)
        predicted = jnp.dot(loadings, states, preferred_element_type=jnp.float32)
        out_ref[:, :, part * slab:(part + 1) * slab] = predicted.astype(out_ref.dtype).reshape(devices, sites, slab)


def call(kernel, name, out_shape, *args, scratch=(), scalars=0, **grid):
    if not grid:
        specs = [pl.BlockSpec(memory_space=pltpu.SMEM)] * scalars
        specs += [pl.BlockSpec(memory_space=pltpu.VMEM)] * (len(args) - scalars)
        grid = dict(in_specs=specs)
    return pl.pallas_call(
        kernel,
        out_shape=out_shape,
        scratch_shapes=list(scratch),
        compiler_params=pltpu.CompilerParams(vmem_limit_bytes=32 << 20),
        name=name,
        **grid,
    )(*args)


def per_device(observations, site_start, site_count, site_gain, site_loading, decay, persistence):
    planes, col, plane = ("zh", "zl"), ("y", "core"), ("x", "y", "core")
    line = plane + ("zl",)
    blocks, parts, nc = lax.axis_size("zh"), lax.axis_size("zl"), lax.axis_size(col)
    devices, slabs = lax.axis_size(plane), lax.axis_size(line)
    sites, epochs = observations.shape
    slab, span = epochs // slabs, epochs // devices
    basis = site_gain.shape[1]
    share = basis // blocks
    f32, bf16 = jnp.float32, jnp.bfloat16
    shape = jax.ShapeDtypeStruct
    turn = [
        ((h * parts + l) * nc + c, (c * parts + l) * nc + h)
        for h in range(blocks) for l in range(parts) for c in range(nc)
    ]

    loadings = lax.all_gather(site_loading, plane, axis=0, tiled=True)

    sent = call(
        front_kernel, "front", shape((devices, sites, span + basis), bf16),
        site_start, site_count, observations, site_gain, grid=(STEPS,),
        in_specs=[pl.BlockSpec(memory_space=pltpu.SMEM)] * 2
        + [pl.BlockSpec((sites, epochs // STEPS), lambda i: (0, i)), pl.BlockSpec((sites, basis), lambda i: (0, 0))],
        out_specs=pl.BlockSpec((devices // STEPS, sites, span + basis), lambda i: (i, 0, 0)),
    )
    got = lax.all_to_all(sent, plane, 0, 0, tiled=True)
    own = lax.dynamic_slice_in_dim(decay, lax.axis_index(col) * share, share, 1)
    decays = lax.ppermute(own, planes + col, turn)
    persist = lax.dynamic_slice_in_dim(persistence, lax.axis_index("zh") * share, share, 0)[None]
    got, decays, persist = lax.optimization_barrier((got, decays, persist))

    partial = call(drive_kernel, "drive", shape((blocks, parts, slab, share), bf16), got)
    summed = lax.all_to_all(partial.reshape(blocks * parts, slab, share), planes, 0, 0, tiled=True)
    summed, loadings = lax.optimization_barrier((summed, loadings))
    square = shape((slab, share), f32)
    smooth, entry, product, summary = call(
        scan_kernel, "scan", (square, square, square, shape((slabs, 8, share), f32)), summed, decays, persist,
        scratch=[pltpu.VMEM((slab, share), f32)],
    )
    summaries = lax.all_to_all(summary, line, 0, 0, tiled=True)
    smoothed, rounded = call(
        finish_kernel, "finish", (square, shape((share, slab), bf16)),
        lax.axis_index(line).astype(jnp.int32)[None], summaries, smooth, entry, product,
        scratch=[pltpu.VMEM((slabs, share), f32)] * 2, scalars=1,
    )

    every = lax.all_gather(rounded, planes, axis=0, tiled=False)
    every, smoothed = lax.optimization_barrier((every, smoothed))
    out = lax.ppermute(smoothed, planes + col, turn)
    predicted = call(
        predict_kernel, "predict", shape((devices, sites, span), bf16),
        loadings, every.reshape(blocks, parts, share, slab), grid=(STEPS,),
        in_specs=[
            pl.BlockSpec((devices * sites // STEPS, basis), lambda i: (i, 0)),
            pl.BlockSpec((blocks, parts, share, slab), lambda i: (0, 0, 0, 0)),
        ],
        out_specs=pl.BlockSpec((devices // STEPS, sites, span), lambda i: (i, 0, 0)),
    )
    back = lax.all_to_all(predicted, plane, 0, 0, tiled=True)
    return (out, back.transpose(1, 0, 2).reshape(sites, epochs))


def solution(mesh):
    fine = Mesh(mesh.devices.reshape(4, 8, 2, 4, 2), ("x", "zh", "zl", "y", "core"))
    tm, col = ("x", "zh", "zl"), ("y", "core")
    every = tm + col
    return jax.shard_map(
        per_device,
        mesh=fine,
        in_specs=(P(every, None), P(every), P(every), P(every, None), P(every, None), P(tm, None), P()),
        out_specs=(P(tm, col), P(every, None)),
        check_vma=False,
    )
```

```python
import jax
import jax.numpy as jnp
from jax import lax
from jax.experimental import pallas as pl
from jax.experimental.pallas import tpu as pltpu
from jax.sharding import Mesh, PartitionSpec as P

ROWS = 8
STEPS = 4


def front_kernel(start_hbm, count_hbm, values_hbm, gain_hbm, out_hbm, start, count, values, gain, out, small, large, sent):
    devices, sites, width = out.shape
    span = width - gain.shape[1]
    wide, each = values.shape[1] // STEPS, devices // STEPS
    arriving = [
        pltpu.make_async_copy(start_hbm, start, small.at[0]),
        pltpu.make_async_copy(count_hbm, count, small.at[1]),
        pltpu.make_async_copy(gain_hbm, gain, small.at[2]),
    ]
    chunks = []
    for step in range(STEPS):
        part = (slice(None), pl.ds(step * wide, wide))
        chunks.append(pltpu.make_async_copy(values_hbm.at[part], values.at[part], large.at[step]))
    for copy in arriving + chunks:
        copy.start()
    for copy in arriving:
        copy.wait()
    site = lax.broadcasted_iota(jnp.int32, (sites, span), 0)
    first = end = jnp.zeros((sites, span), jnp.int32)
    for s in range(sites):
        first = jnp.where(site == s, start[s], first)
        end = jnp.where(site == s, start[s] + count[s], end)
    epoch = lax.broadcasted_iota(jnp.int32, (sites, span), 1)
    gains = gain[...]
    leaving = []
    for step in range(STEPS):
        chunks[step].wait()
        for to in range(step * each, (step + 1) * each):
            own = values[:, to * span:(to + 1) * span].astype(jnp.float32)
            inside = (epoch + to * span >= first) & (epoch + to * span < end)
            out[to, :, :span] = jnp.where(inside, own, 0.0).astype(out.dtype)
            out[to, :, span:] = gains
        part = pl.ds(step * each, each)
        leaving.append(pltpu.make_async_copy(out.at[part], out_hbm.at[part], sent.at[step]))
        leaving[-1].start()
    for copy in leaving:
        copy.wait()


def drive_kernel(got_ref, out_ref):
    sources, sites, _ = got_ref.shape
    blocks, parts, slab, share = out_ref.shape
    span = parts * slab
    rows = got_ref[:, :, :span].reshape(sources * sites, span)
    gains = got_ref[:, :, span:].reshape(sources * sites, blocks * share)
    partial = lax.dot_general(rows, gains, (((0,), (0,)), ((), ())), preferred_element_type=jnp.float32)
    partial = partial.astype(out_ref.dtype)
    for block in range(blocks):
        for part in range(parts):
            out_ref[block, part] = partial[part * slab:(part + 1) * slab, block * share:(block + 1) * share]


def shifted(value, by, fill):
    count = value.shape[0]
    row = lax.broadcasted_iota(jnp.int32, value.shape, 0)
    moved = pltpu.roll(value, by % count, 0)
    inside = row >= by if by > 0 else row < count + by
    return jnp.where(inside, moved, fill)


def across(rate, states, sign):
    step = 1
    while step < ROWS:
        states = [s + rate * shifted(s, sign * step, 0.0) for s in states]
        rate = rate * shifted(rate, sign * step, 1.0)
        step *= 2
    return shifted(rate, sign, 1.0), [shifted(s, sign, 0.0) for s in states]


def scan_kernel(parts_ref, decay_ref, persist_ref, smooth_ref, entry_ref, product_ref, summary_ref, inj):
    sources, slab, width = parts_ref.shape
    total = parts_ref[0].astype(jnp.float32)
    for source in range(1, sources):
        total = total + parts_ref[source].astype(jnp.float32)
    inj[...] = jnp.sqrt(1.0 - decay_ref[...] * decay_ref[...]) * total
    depth = slab // ROWS
    persist = persist_ref[...]

    def rows(ref, j):
        return ref[pl.ds(j, ROWS, stride=depth), :]

    decays = [rows(decay_ref, j) for j in range(depth)]
    decayed, local = [decays[0]], [rows(inj, 0)]
    for j in range(1, depth):
        decayed.append(decays[j] * decayed[-1])
        local.append(decays[j] * local[-1] + rows(inj, j))
    enter_rate, (enter,) = across(decayed[-1], [local[-1]], 1)
    local = [h + a * enter for h, a in zip(local, decayed)]
    decayed = [a * enter_rate for a in decayed]
    products, smooth, entry = [None] * depth, [None] * depth, [None] * depth
    for j in reversed(range(depth)):
        rate = persist * decays[j]
        keep = 1.0 - rate * decays[j]
        if j == depth - 1:
            products[j], smooth[j], entry[j] = rate, keep * local[j], keep * decayed[j]
        else:
            products[j] = rate * products[j + 1]
            smooth[j] = rate * smooth[j + 1] + keep * local[j]
            entry[j] = rate * entry[j + 1] + keep * decayed[j]
    leave_rate, (leave_smooth, leave_entry) = across(products[0], [smooth[0], entry[0]], -1)
    for j in range(depth):
        smooth[j] = smooth[j] + products[j] * leave_smooth
        entry[j] = entry[j] + products[j] * leave_entry
        products[j] = products[j] * leave_rate
        smooth_ref[pl.ds(j, ROWS, stride=depth), :] = smooth[j]
        entry_ref[pl.ds(j, ROWS, stride=depth), :] = entry[j]
        product_ref[pl.ds(j, ROWS, stride=depth), :] = products[j]
    summary = [decayed[-1][ROWS - 1:], local[-1][ROWS - 1:], products[0][:1], smooth[0][:1], entry[0][:1]]
    summary = jnp.concatenate(summary + [jnp.zeros((3, width), jnp.float32)], axis=0)
    for to in range(summary_ref.shape[0]):
        summary_ref[to] = summary


def finish_kernel(place_ref, slabs_ref, smooth_ref, entry_ref, product_ref, rounded_ref, fwd, bwd):
    count, _, width = slabs_ref.shape

    def of(at, what):
        return slabs_ref[at, what:what + 1, :]

    state = jnp.zeros((1, width), jnp.float32)
    for at in range(count):
        fwd[at:at + 1, :] = state
        state = of(at, 0) * state + of(at, 1)
    state = jnp.zeros((1, width), jnp.float32)
    for at in reversed(range(count)):
        bwd[at:at + 1, :] = state
        state = of(at, 2) * state + (of(at, 3) + of(at, 4) * fwd[at:at + 1, :])
    place = place_ref[0]
    f_in, g_in = fwd[pl.ds(place, 1), :], bwd[pl.ds(place, 1), :]
    smoothed = smooth_ref[...] + entry_ref[...] * f_in + product_ref[...] * g_in
    rounded_ref[...] = smoothed.T.astype(rounded_ref.dtype)


def predict_kernel(where_ref, near_ref, far_ref, rounded_ref, out_ref, own_ref):
    blocks, parts, share, slab = rounded_ref.shape
    pairs, _, sites, _ = out_ref.shape
    part, y, core = where_ref[0], where_ref[1], where_ref[2]
    loadings = jnp.concatenate([near_ref[...], far_ref[...]], axis=0)
    for at in range(parts):
        states = rounded_ref[:, at].reshape(blocks * share, slab)
        predicted = jnp.dot(loadings, states, preferred_element_type=jnp.float32).astype(out_ref.dtype)
        predicted = predicted.reshape(2, pairs, sites, slab)
        for other in range(2):
            out_ref[:, core ^ other, :, at * slab:(at + 1) * slab] = predicted[other]
    for other in range(own_ref.shape[1]):
        own_ref[0, other] = rounded_ref[(y ^ pl.program_id(0)) * own_ref.shape[1] + (core ^ other), part]


def call(kernel, name, out_shape, *args, scratch=(), scalars=0, vmem=32, **grid):
    if "in_specs" not in grid:
        specs = [pl.BlockSpec(memory_space=pltpu.SMEM)] * scalars
        specs += [pl.BlockSpec(memory_space=pltpu.VMEM)] * (len(args) - scalars)
        grid = dict(in_specs=specs)
    return pl.pallas_call(
        kernel,
        out_shape=out_shape,
        scratch_shapes=list(scratch),
        compiler_params=pltpu.CompilerParams(vmem_limit_bytes=vmem << 20),
        name=name,
        **grid,
    )(*args)


def per_device(observations, site_start, site_count, site_gain, site_loading, decay, persistence):
    planes, col, plane = ("zh", "zl"), ("y", "core"), ("x", "y", "core")
    line = plane + ("zl",)
    blocks, parts, nc = lax.axis_size("zh"), lax.axis_size("zl"), lax.axis_size(col)
    devices, slabs = lax.axis_size(plane), lax.axis_size(line)
    sites, epochs = observations.shape
    slab, span = epochs // slabs, epochs // devices
    basis = site_gain.shape[1]
    share = basis // blocks
    f32, bf16 = jnp.float32, jnp.bfloat16
    shape = jax.ShapeDtypeStruct
    turn = [
        ((h * parts + l) * nc + c, (c * parts + l) * nc + h)
        for h in range(blocks) for l in range(parts) for c in range(nc)
    ]

    hbm, smem = pl.BlockSpec(memory_space=pl.ANY), pltpu.SMEM
    sent = call(
        front_kernel, "front", shape((devices, sites, span + basis), bf16),
        site_start, site_count, observations, site_gain, in_specs=[hbm] * 4, out_specs=hbm, vmem=60,
        scratch=[
            smem((sites,), jnp.int32), smem((sites,), jnp.int32),
            pltpu.VMEM((sites, epochs), bf16), pltpu.VMEM((sites, basis), bf16),
            pltpu.VMEM((devices, sites, span + basis), bf16),
            pltpu.SemaphoreType.DMA((3,)), pltpu.SemaphoreType.DMA((STEPS,)), pltpu.SemaphoreType.DMA((STEPS,)),
        ],
    )
    got = lax.all_to_all(sent, plane, 0, 0, tiled=True)
    own = lax.dynamic_slice_in_dim(decay, lax.axis_index(col) * share, share, 1)
    decays = lax.ppermute(own, planes + col, turn)
    persist = lax.dynamic_slice_in_dim(persistence, lax.axis_index("zh") * share, share, 0)[None]
    got, decays, persist = lax.optimization_barrier((got, decays, persist))
    loadings, got = lax.optimization_barrier((site_loading, got))
    near = lax.all_gather(loadings, ("x", "y"), axis=0, tiled=True)

    partial = call(drive_kernel, "drive", shape((blocks, parts, slab, share), bf16), got)
    summed = lax.all_to_all(partial.reshape(blocks * parts, slab, share), planes, 0, 0, tiled=True)
    summed, near = lax.optimization_barrier((summed, near))
    far = lax.ppermute(near, "core", [(0, 1), (1, 0)])
    square = shape((slab, share), f32)
    smooth, entry, product, summary = call(
        scan_kernel, "scan", (square, square, square, shape((slabs, 8, share), f32)), summed, decays, persist,
        scratch=[pltpu.VMEM((slab, share), f32)],
    )
    summaries = lax.all_to_all(summary, line, 0, 0, tiled=True)
    rounded = call(
        finish_kernel, "finish", shape((share, slab), bf16),
        lax.axis_index(line).astype(jnp.int32)[None], summaries, smooth, entry, product,
        scratch=[pltpu.VMEM((slabs, share), f32)] * 2, scalars=1,
    )

    every = lax.all_gather(rounded, planes, axis=0, tiled=False)
    ny, cores = lax.axis_size("y"), lax.axis_size("core")
    y, core = lax.axis_index("y"), lax.axis_index("core")
    rows = near.shape[0] // ny
    predicted, own = call(
        predict_kernel, "predict",
        (shape((devices // cores, cores, sites, span), bf16), shape((ny, cores, share, slab), bf16)),
        jnp.stack([lax.axis_index("zl"), y, core]).astype(jnp.int32), near, far,
        every.reshape(blocks, parts, share, slab), grid=(ny,),
        in_specs=[
            pl.BlockSpec(memory_space=smem),
            pl.BlockSpec((rows, basis), lambda i: (i, 0)),
            pl.BlockSpec((rows, basis), lambda i: (i, 0)),
            pl.BlockSpec((blocks, parts, share, slab), lambda i: (0, 0, 0, 0)),
        ],
        out_specs=(
            pl.BlockSpec((devices // cores // ny, cores, sites, span), lambda i: (i, 0, 0, 0)),
            pl.BlockSpec((1, cores, share, slab), lambda i: (i, 0, 0, 0)),
        ),
    )
    back = lax.all_to_all(predicted.reshape(devices, sites, span), plane, 0, 0, tiled=True)
    holder = lax.axis_index("zh")
    got = own[0]
    for step in range(1, ny):
        moved = lax.ppermute(own[step], "y", [(i, i ^ step) for i in range(ny)])
        got = jnp.where((holder // cores) ^ y == step, moved, got)
    swapped = lax.ppermute(got[1], "core", [(0, 1), (1, 0)])
    out = jnp.where(holder % cores == core, got[0], swapped).T.astype(f32)
    return (out, back.transpose(1, 0, 2).reshape(sites, epochs))


def solution(mesh):
    fine = Mesh(mesh.devices.reshape(4, 8, 2, 4, 2), ("x", "zh", "zl", "y", "core"))
    tm, col = ("x", "zh", "zl"), ("y", "core")
    every = tm + col
    return jax.shard_map(
        per_device,
        mesh=fine,
        in_specs=(P(every, None), P(every), P(every), P(every, None), P(every, None), P(tm, None), P()),
        out_specs=(P(tm, col), P(every, None)),
        check_vma=False,
    )
```

```python
import jax
import jax.numpy as jnp
from jax import lax
from jax.experimental import pallas as pl
from jax.experimental.pallas import tpu as pltpu
from jax.sharding import Mesh, PartitionSpec as P

ROWS = 8
STEPS = 4


def front_kernel(start_hbm, count_hbm, values_hbm, gain_hbm, out_hbm, start, count, values, gain, out, small, large, sent):
    devices, sites, width = out.shape
    span = width - gain.shape[1]
    wide, each = values.shape[1] // STEPS, devices // STEPS
    arriving = [
        pltpu.make_async_copy(start_hbm, start, small.at[0]),
        pltpu.make_async_copy(count_hbm, count, small.at[1]),
        pltpu.make_async_copy(gain_hbm, gain, small.at[2]),
    ]
    chunks = []
    for step in range(STEPS):
        part = (slice(None), pl.ds(step * wide, wide))
        chunks.append(pltpu.make_async_copy(values_hbm.at[part], values.at[part], large.at[step]))
    for copy in arriving + chunks:
        copy.start()
    for copy in arriving:
        copy.wait()
    site = lax.broadcasted_iota(jnp.int32, (sites, span), 0)
    first = end = jnp.zeros((sites, span), jnp.int32)
    for s in range(sites):
        first = jnp.where(site == s, start[s], first)
        end = jnp.where(site == s, start[s] + count[s], end)
    epoch = lax.broadcasted_iota(jnp.int32, (sites, span), 1)
    gains = gain[...]
    leaving = []
    for step in range(STEPS):
        chunks[step].wait()
        for to in range(step * each, (step + 1) * each):
            own = values[:, to * span:(to + 1) * span].astype(jnp.float32)
            inside = (epoch + to * span >= first) & (epoch + to * span < end)
            out[to, :, :span] = jnp.where(inside, own, 0.0).astype(out.dtype)
            out[to, :, span:] = gains
        part = pl.ds(step * each, each)
        leaving.append(pltpu.make_async_copy(out.at[part], out_hbm.at[part], sent.at[step]))
        leaving[-1].start()
    for copy in leaving:
        copy.wait()


def drive_kernel(got_ref, out_ref):
    sources, sites, _ = got_ref.shape
    blocks, parts, slab, share = out_ref.shape
    span = parts * slab
    rows = got_ref[:, :, :span].reshape(sources * sites, span)
    gains = got_ref[:, :, span:].reshape(sources * sites, blocks * share)
    partial = lax.dot_general(rows, gains, (((0,), (0,)), ((), ())), preferred_element_type=jnp.float32)
    partial = partial.astype(out_ref.dtype)
    for block in range(blocks):
        for part in range(parts):
            out_ref[block, part] = partial[part * slab:(part + 1) * slab, block * share:(block + 1) * share]


def shifted(value, by, fill):
    count = value.shape[0]
    row = lax.broadcasted_iota(jnp.int32, value.shape, 0)
    moved = pltpu.roll(value, by % count, 0)
    inside = row >= by if by > 0 else row < count + by
    return jnp.where(inside, moved, fill)


def across(rate, states, sign):
    step = 1
    while step < ROWS:
        states = [s + rate * shifted(s, sign * step, 0.0) for s in states]
        rate = rate * shifted(rate, sign * step, 1.0)
        step *= 2
    return shifted(rate, sign, 1.0), [shifted(s, sign, 0.0) for s in states]


def scan_kernel(parts_ref, decay_ref, persist_ref, smooth_ref, entry_ref, product_ref, summary_ref, inj):
    sources, slab, width = parts_ref.shape
    total = parts_ref[0].astype(jnp.float32)
    for source in range(1, sources):
        total = total + parts_ref[source].astype(jnp.float32)
    inj[...] = jnp.sqrt(1.0 - decay_ref[...] * decay_ref[...]) * total
    depth = slab // ROWS
    persist = persist_ref[...]

    def rows(ref, j):
        return ref[pl.ds(j, ROWS, stride=depth), :]

    decays = [rows(decay_ref, j) for j in range(depth)]
    decayed, local = [decays[0]], [rows(inj, 0)]
    for j in range(1, depth):
        decayed.append(decays[j] * decayed[-1])
        local.append(decays[j] * local[-1] + rows(inj, j))
    enter_rate, (enter,) = across(decayed[-1], [local[-1]], 1)
    local = [h + a * enter for h, a in zip(local, decayed)]
    decayed = [a * enter_rate for a in decayed]
    products, smooth, entry = [None] * depth, [None] * depth, [None] * depth
    for j in reversed(range(depth)):
        rate = persist * decays[j]
        keep = 1.0 - rate * decays[j]
        if j == depth - 1:
            products[j], smooth[j], entry[j] = rate, keep * local[j], keep * decayed[j]
        else:
            products[j] = rate * products[j + 1]
            smooth[j] = rate * smooth[j + 1] + keep * local[j]
            entry[j] = rate * entry[j + 1] + keep * decayed[j]
    leave_rate, (leave_smooth, leave_entry) = across(products[0], [smooth[0], entry[0]], -1)
    for j in range(depth):
        smooth[j] = smooth[j] + products[j] * leave_smooth
        entry[j] = entry[j] + products[j] * leave_entry
        products[j] = products[j] * leave_rate
        smooth_ref[pl.ds(j, ROWS, stride=depth), :] = smooth[j]
        entry_ref[pl.ds(j, ROWS, stride=depth), :] = entry[j]
        product_ref[pl.ds(j, ROWS, stride=depth), :] = products[j]
    summary = [decayed[-1][ROWS - 1:], local[-1][ROWS - 1:], products[0][:1], smooth[0][:1], entry[0][:1]]
    summary = jnp.concatenate(summary + [jnp.zeros((3, width), jnp.float32)], axis=0)
    for to in range(summary_ref.shape[0]):
        summary_ref[to] = summary


def finish_kernel(place_ref, slabs_ref, smooth_ref, entry_ref, product_ref, rounded_ref, fwd, bwd):
    count, _, width = slabs_ref.shape

    def of(at, what):
        return slabs_ref[at, what:what + 1, :]

    state = jnp.zeros((1, width), jnp.float32)
    for at in range(count):
        fwd[at:at + 1, :] = state
        state = of(at, 0) * state + of(at, 1)
    state = jnp.zeros((1, width), jnp.float32)
    for at in reversed(range(count)):
        bwd[at:at + 1, :] = state
        state = of(at, 2) * state + (of(at, 3) + of(at, 4) * fwd[at:at + 1, :])
    place = place_ref[0]
    f_in, g_in = fwd[pl.ds(place, 1), :], bwd[pl.ds(place, 1), :]
    smoothed = smooth_ref[...] + entry_ref[...] * f_in + product_ref[...] * g_in
    rounded_ref[...] = smoothed.T.astype(rounded_ref.dtype)


def predict_kernel(where_ref, near_ref, far_ref, mine_ref, pair_ref, out_ref):
    blocks, share, slab = mine_ref.shape
    pairs, _, sites, _ = out_ref.shape
    part, core = where_ref[0], where_ref[1]
    loadings = jnp.concatenate([near_ref[...], far_ref[...]], axis=0)
    predicted = []
    for ref in (mine_ref, pair_ref):
        states = ref[...].reshape(blocks * share, slab)
        predicted.append(jnp.dot(loadings, states, preferred_element_type=jnp.float32))
    mine, pair = predicted
    for at in range(2):
        chosen = jnp.where(part == at, mine, pair).astype(out_ref.dtype).reshape(2, pairs, sites, slab)
        for other in range(2):
            out_ref[:, core ^ other, :, at * slab:(at + 1) * slab] = chosen[other]


def call(kernel, name, out_shape, *args, scratch=(), scalars=0, vmem=32, **grid):
    if "in_specs" not in grid:
        specs = [pl.BlockSpec(memory_space=pltpu.SMEM)] * scalars
        specs += [pl.BlockSpec(memory_space=pltpu.VMEM)] * (len(args) - scalars)
        grid = dict(in_specs=specs)
    return pl.pallas_call(
        kernel,
        out_shape=out_shape,
        scratch_shapes=list(scratch),
        compiler_params=pltpu.CompilerParams(vmem_limit_bytes=vmem << 20),
        name=name,
        **grid,
    )(*args)


def per_device(observations, site_start, site_count, site_gain, site_loading, decay, persistence):
    planes, col, plane = ("zh", "zl"), ("y", "core"), ("x", "y", "core")
    line = plane + ("zl",)
    blocks, parts, nc = lax.axis_size("zh"), lax.axis_size("zl"), lax.axis_size(col)
    devices, slabs = lax.axis_size(plane), lax.axis_size(line)
    sites, epochs = observations.shape
    slab, span = epochs // slabs, epochs // devices
    basis = site_gain.shape[1]
    share = basis // blocks
    f32, bf16 = jnp.float32, jnp.bfloat16
    shape = jax.ShapeDtypeStruct
    turn = [
        ((h * parts + l) * nc + c, (c * parts + l) * nc + h)
        for h in range(blocks) for l in range(parts) for c in range(nc)
    ]

    hbm, smem = pl.BlockSpec(memory_space=pl.ANY), pltpu.SMEM
    sent = call(
        front_kernel, "front", shape((devices, sites, span + basis), bf16),
        site_start, site_count, observations, site_gain, in_specs=[hbm] * 4, out_specs=hbm, vmem=60,
        scratch=[
            smem((sites,), jnp.int32), smem((sites,), jnp.int32),
            pltpu.VMEM((sites, epochs), bf16), pltpu.VMEM((sites, basis), bf16),
            pltpu.VMEM((devices, sites, span + basis), bf16),
            pltpu.SemaphoreType.DMA((3,)), pltpu.SemaphoreType.DMA((STEPS,)), pltpu.SemaphoreType.DMA((STEPS,)),
        ],
    )
    got = lax.all_to_all(sent, plane, 0, 0, tiled=True)
    own = lax.dynamic_slice_in_dim(decay, lax.axis_index(col) * share, share, 1)
    decays = lax.ppermute(own, planes + col, turn)
    persist = lax.dynamic_slice_in_dim(persistence, lax.axis_index("zh") * share, share, 0)[None]
    got, decays, persist = lax.optimization_barrier((got, decays, persist))
    loadings, got = lax.optimization_barrier((site_loading, got))
    near = lax.all_gather(loadings, ("x", "y"), axis=0, tiled=True)

    partial = call(drive_kernel, "drive", shape((blocks, parts, slab, share), bf16), got)
    summed = lax.all_to_all(partial.reshape(blocks * parts, slab, share), planes, 0, 0, tiled=True)
    summed, near = lax.optimization_barrier((summed, near))
    far = lax.ppermute(near, "core", [(0, 1), (1, 0)])
    square = shape((slab, share), f32)
    smooth, entry, product, summary = call(
        scan_kernel, "scan", (square, square, square, shape((slabs, 8, share), f32)), summed, decays, persist,
        scratch=[pltpu.VMEM((slab, share), f32)],
    )
    summaries = lax.all_to_all(summary, line, 0, 0, tiled=True)
    rounded = call(
        finish_kernel, "finish", shape((share, slab), bf16),
        lax.axis_index(line).astype(jnp.int32)[None], summaries, smooth, entry, product,
        scratch=[pltpu.VMEM((slabs, share), f32)] * 2, scalars=1,
    )

    mine = lax.all_gather(rounded, "zh", axis=0, tiled=False)
    pair = lax.ppermute(mine, "zl", [(0, 1), (1, 0)])
    own = lax.all_to_all(mine, col, 0, 0, tiled=True)
    pair, own = lax.optimization_barrier((pair, own))
    out = lax.dynamic_index_in_dim(own, lax.axis_index("zh"), 0, False).T.astype(f32)

    cores = lax.axis_size("core")
    where = jnp.stack([lax.axis_index("zl"), lax.axis_index("core")]).astype(jnp.int32)
    whole = pl.BlockSpec((blocks, share, slab), lambda i: (0, 0, 0))
    rows = pl.BlockSpec((near.shape[0] // STEPS, basis), lambda i: (i, 0))
    predicted = call(
        predict_kernel, "predict", shape((devices // cores, cores, sites, span), bf16),
        where, near, far, mine, pair, grid=(STEPS,),
        in_specs=[pl.BlockSpec(memory_space=smem), rows, rows, whole, whole],
        out_specs=pl.BlockSpec((devices // cores // STEPS, cores, sites, span), lambda i: (i, 0, 0, 0)),
    )
    back = lax.all_to_all(predicted.reshape(devices, sites, span), plane, 0, 0, tiled=True)
    return (out, back.transpose(1, 0, 2).reshape(sites, epochs))


def solution(mesh):
    fine = Mesh(mesh.devices.reshape(4, 8, 2, 4, 2), ("x", "zh", "zl", "y", "core"))
    tm, col = ("x", "zh", "zl"), ("y", "core")
    every = tm + col
    return jax.shard_map(
        per_device,
        mesh=fine,
        in_specs=(P(every, None), P(every), P(every), P(every, None), P(every, None), P(tm, None), P()),
        out_specs=(P(tm, col), P(every, None)),
        check_vma=False,
    )
```

```python
import jax
import jax.numpy as jnp
from jax import lax
from jax.experimental import pallas as pl
from jax.experimental.pallas import tpu as pltpu
from jax.sharding import Mesh, PartitionSpec as P

ROWS = 8
STEPS = 4


def front_kernel(start_hbm, count_hbm, values_hbm, gain_hbm, out_hbm, start, count, values, gain, out, small, large, sent):
    devices, sites, width = out.shape
    span = width - gain.shape[1]
    wide, each = values.shape[1] // STEPS, devices // STEPS
    arriving = [
        pltpu.make_async_copy(start_hbm, start, small.at[0]),
        pltpu.make_async_copy(count_hbm, count, small.at[1]),
        pltpu.make_async_copy(gain_hbm, gain, small.at[2]),
    ]
    chunks = []
    for step in range(STEPS):
        part = (slice(None), pl.ds(step * wide, wide))
        chunks.append(pltpu.make_async_copy(values_hbm.at[part], values.at[part], large.at[step]))
    for copy in arriving + chunks:
        copy.start()
    for copy in arriving:
        copy.wait()
    site = lax.broadcasted_iota(jnp.int32, (sites, span), 0)
    first = end = jnp.zeros((sites, span), jnp.int32)
    for s in range(sites):
        first = jnp.where(site == s, start[s], first)
        end = jnp.where(site == s, start[s] + count[s], end)
    epoch = lax.broadcasted_iota(jnp.int32, (sites, span), 1)
    gains = gain[...]
    leaving = []
    for step in range(STEPS):
        chunks[step].wait()
        for to in range(step * each, (step + 1) * each):
            own = values[:, to * span:(to + 1) * span].astype(jnp.float32)
            inside = (epoch + to * span >= first) & (epoch + to * span < end)
            out[to, :, :span] = jnp.where(inside, own, 0.0).astype(out.dtype)
            out[to, :, span:] = gains
        part = pl.ds(step * each, each)
        leaving.append(pltpu.make_async_copy(out.at[part], out_hbm.at[part], sent.at[step]))
        leaving[-1].start()
    for copy in leaving:
        copy.wait()


def drive_kernel(part_ref, got_ref, keep_ref, give_ref):
    sources, sites, width = got_ref.shape
    blocks, slab, share = keep_ref.shape
    span = width - blocks * share
    rows = got_ref[:, :, :span].reshape(sources * sites, span)
    gains = got_ref[:, :, span:].reshape(sources * sites, blocks * share)
    partial = lax.dot_general(rows, gains, (((0,), (0,)), ((), ())), preferred_element_type=jnp.float32)
    first = part_ref[0] == 0
    keep = jnp.where(first, partial[:slab], partial[slab:])
    give = jnp.where(first, partial[slab:], partial[:slab]).astype(give_ref.dtype)
    for block in range(blocks):
        keep_ref[block] = keep[:, block * share:(block + 1) * share]
        give_ref[block] = give[:, block * share:(block + 1) * share]


def shifted(value, by, fill):
    count = value.shape[0]
    row = lax.broadcasted_iota(jnp.int32, value.shape, 0)
    moved = pltpu.roll(value, by % count, 0)
    inside = row >= by if by > 0 else row < count + by
    return jnp.where(inside, moved, fill)


def across(rate, states, sign):
    step = 1
    while step < ROWS:
        states = [s + rate * shifted(s, sign * step, 0.0) for s in states]
        rate = rate * shifted(rate, sign * step, 1.0)
        step *= 2
    return shifted(rate, sign, 1.0), [shifted(s, sign, 0.0) for s in states]


def scan_kernel(parts_ref, decay_ref, persist_ref, smooth_ref, entry_ref, product_ref, summary_ref, inj):
    sources, slab, width = parts_ref.shape
    total = parts_ref[0].astype(jnp.float32)
    for source in range(1, sources):
        total = total + parts_ref[source].astype(jnp.float32)
    inj[...] = jnp.sqrt(1.0 - decay_ref[...] * decay_ref[...]) * total
    depth = slab // ROWS
    persist = persist_ref[...]

    def rows(ref, j):
        return ref[pl.ds(j, ROWS, stride=depth), :]

    decays = [rows(decay_ref, j) for j in range(depth)]
    decayed, local = [decays[0]], [rows(inj, 0)]
    for j in range(1, depth):
        decayed.append(decays[j] * decayed[-1])
        local.append(decays[j] * local[-1] + rows(inj, j))
    enter_rate, (enter,) = across(decayed[-1], [local[-1]], 1)
    local = [h + a * enter for h, a in zip(local, decayed)]
    decayed = [a * enter_rate for a in decayed]
    products, smooth, entry = [None] * depth, [None] * depth, [None] * depth
    for j in reversed(range(depth)):
        rate = persist * decays[j]
        keep = 1.0 - rate * decays[j]
        if j == depth - 1:
            products[j], smooth[j], entry[j] = rate, keep * local[j], keep * decayed[j]
        else:
            products[j] = rate * products[j + 1]
            smooth[j] = rate * smooth[j + 1] + keep * local[j]
            entry[j] = rate * entry[j + 1] + keep * decayed[j]
    leave_rate, (leave_smooth, leave_entry) = across(products[0], [smooth[0], entry[0]], -1)
    for j in range(depth):
        smooth[j] = smooth[j] + products[j] * leave_smooth
        entry[j] = entry[j] + products[j] * leave_entry
        products[j] = products[j] * leave_rate
        smooth_ref[pl.ds(j, ROWS, stride=depth), :] = smooth[j]
        entry_ref[pl.ds(j, ROWS, stride=depth), :] = entry[j]
        product_ref[pl.ds(j, ROWS, stride=depth), :] = products[j]
    summary = [decayed[-1][ROWS - 1:], local[-1][ROWS - 1:], products[0][:1], smooth[0][:1], entry[0][:1]]
    summary = jnp.concatenate(summary + [jnp.zeros((3, width), jnp.float32)], axis=0)
    for to in range(summary_ref.shape[0]):
        summary_ref[to] = summary


def finish_kernel(place_ref, slabs_ref, smooth_ref, entry_ref, product_ref, rounded_ref, fwd, bwd):
    count, _, width = slabs_ref.shape

    def of(at, what):
        return slabs_ref[at, what:what + 1, :]

    state = jnp.zeros((1, width), jnp.float32)
    for at in range(count):
        fwd[at:at + 1, :] = state
        state = of(at, 0) * state + of(at, 1)
    state = jnp.zeros((1, width), jnp.float32)
    for at in reversed(range(count)):
        bwd[at:at + 1, :] = state
        state = of(at, 2) * state + (of(at, 3) + of(at, 4) * fwd[at:at + 1, :])
    place = place_ref[0]
    f_in, g_in = fwd[pl.ds(place, 1), :], bwd[pl.ds(place, 1), :]
    smoothed = smooth_ref[...] + entry_ref[...] * f_in + product_ref[...] * g_in
    rounded = smoothed.T.astype(rounded_ref.dtype)
    for to in range(rounded_ref.shape[0]):
        rounded_ref[to] = rounded


def predict_kernel(where_ref, near_ref, far_ref, mine_ref, pair_ref, out_ref):
    blocks, share, slab = mine_ref.shape
    pairs, _, sites, span = out_ref.shape
    first, core = where_ref[0] == 0, where_ref[1]
    mine, pair = mine_ref[...].reshape(blocks * share, slab), pair_ref[...].reshape(blocks * share, slab)
    states = jnp.concatenate([jnp.where(first, mine, pair), jnp.where(first, pair, mine)], axis=1)
    loadings = jnp.concatenate([near_ref[...], far_ref[...]], axis=0)
    predicted = jnp.dot(loadings, states, preferred_element_type=jnp.float32)
    predicted = predicted.astype(out_ref.dtype).reshape(2, pairs, sites, span)
    for other in range(2):
        out_ref[:, core ^ other] = predicted[other]


def call(kernel, name, out_shape, *args, scratch=(), scalars=0, vmem=32, **grid):
    if "in_specs" not in grid:
        specs = [pl.BlockSpec(memory_space=pltpu.SMEM)] * scalars
        specs += [pl.BlockSpec(memory_space=pltpu.VMEM)] * (len(args) - scalars)
        grid = dict(in_specs=specs)
    return pl.pallas_call(
        kernel,
        out_shape=out_shape,
        scratch_shapes=list(scratch),
        compiler_params=pltpu.CompilerParams(vmem_limit_bytes=vmem << 20),
        name=name,
        **grid,
    )(*args)


def per_device(observations, site_start, site_count, site_gain, site_loading, decay, persistence):
    planes, col, plane = ("zh", "zl"), ("y", "core"), ("x", "y", "core")
    line = plane + ("zl",)
    blocks, parts, nc = lax.axis_size("zh"), lax.axis_size("zl"), lax.axis_size(col)
    devices, slabs = lax.axis_size(plane), lax.axis_size(line)
    sites, epochs = observations.shape
    slab, span = epochs // slabs, epochs // devices
    basis = site_gain.shape[1]
    share = basis // blocks
    f32, bf16 = jnp.float32, jnp.bfloat16
    shape = jax.ShapeDtypeStruct
    turn = [
        ((h * parts + l) * nc + c, (c * parts + l) * nc + h)
        for h in range(blocks) for l in range(parts) for c in range(nc)
    ]

    hbm, smem = pl.BlockSpec(memory_space=pl.ANY), pltpu.SMEM
    sent = call(
        front_kernel, "front", shape((devices, sites, span + basis), bf16),
        site_start, site_count, observations, site_gain, in_specs=[hbm] * 4, out_specs=hbm, vmem=60,
        scratch=[
            smem((sites,), jnp.int32), smem((sites,), jnp.int32),
            pltpu.VMEM((sites, epochs), bf16), pltpu.VMEM((sites, basis), bf16),
            pltpu.VMEM((devices, sites, span + basis), bf16),
            pltpu.SemaphoreType.DMA((3,)), pltpu.SemaphoreType.DMA((STEPS,)), pltpu.SemaphoreType.DMA((STEPS,)),
        ],
    )
    got = lax.all_to_all(sent, plane, 0, 0, tiled=True)
    own = lax.dynamic_slice_in_dim(decay, lax.axis_index(col) * share, share, 1)
    decays = lax.ppermute(own, planes + col, turn)
    persist = lax.dynamic_slice_in_dim(persistence, lax.axis_index("zh") * share, share, 0)[None]
    got, decays, persist = lax.optimization_barrier((got, decays, persist))

    part = lax.axis_index("zl").astype(jnp.int32)
    both = (shape((blocks, slab, share), f32), shape((blocks, slab, share), bf16))
    keep, give = call(drive_kernel, "drive", both, part[None], got, scalars=1)
    taken = lax.ppermute(give, "zl", [(0, 1), (1, 0)])
    taken, near = lax.optimization_barrier((taken, site_loading))
    halves = (keep + taken.astype(f32)).astype(bf16)
    summed = lax.all_to_all(halves, "zh", 0, 0, tiled=True)
    near = lax.all_gather(near, "y", axis=0, tiled=True)
    summed, near = lax.optimization_barrier((summed, near))
    square = shape((slab, share), f32)
    smooth, entry, product, summary = call(
        scan_kernel, "scan", (square, square, square, shape((slabs, 8, share), f32)), summed, decays, persist,
        scratch=[pltpu.VMEM((slab, share), f32)],
    )
    summaries = lax.all_to_all(summary, line, 0, 0, tiled=True)
    summaries, near = lax.optimization_barrier((summaries, near))
    rounded = call(
        finish_kernel, "finish", shape((blocks, share, slab), bf16),
        lax.axis_index(line).astype(jnp.int32)[None], summaries, smooth, entry, product,
        scratch=[pltpu.VMEM((slabs, share), f32)] * 2, scalars=1,
    )

    mine = lax.all_to_all(rounded, "zh", 0, 0, tiled=True)
    near = lax.all_gather(near, "x", axis=0, tiled=True)
    mine, near = lax.optimization_barrier((mine, near))
    far = lax.ppermute(near, "core", [(0, 1), (1, 0)])
    pair = lax.ppermute(mine, "zl", [(0, 1), (1, 0)])
    own = lax.all_to_all(mine, col, 0, 0, tiled=True)

    cores = lax.axis_size("core")
    where = jnp.stack([part, lax.axis_index("core").astype(jnp.int32)])
    predicted = call(
        predict_kernel, "predict", shape((devices // cores, cores, sites, span), bf16),
        where, near, far, mine, pair, scalars=1,
    )
    predicted, own = lax.optimization_barrier((predicted, own))
    out = lax.dynamic_index_in_dim(own, lax.axis_index("zh"), 0, False).T.astype(f32)
    back = lax.all_to_all(predicted.reshape(devices, sites, span), plane, 0, 0, tiled=True)
    return (out, back.transpose(1, 0, 2).reshape(sites, epochs))


def solution(mesh):
    fine = Mesh(mesh.devices.reshape(4, 8, 2, 4, 2), ("x", "zh", "zl", "y", "core"))
    tm, col = ("x", "zh", "zl"), ("y", "core")
    every = tm + col
    return jax.shard_map(
        per_device,
        mesh=fine,
        in_specs=(P(every, None), P(every), P(every), P(every, None), P(every, None), P(tm, None), P()),
        out_specs=(P(tm, col), P(every, None)),
        check_vma=False,
    )
```

```python
import jax
import jax.numpy as jnp
from jax import lax
from jax.experimental import pallas as pl
from jax.experimental.pallas import tpu as pltpu
from jax.sharding import Mesh, PartitionSpec as P

ROWS = 8
STEPS = 4


def front_kernel(start_hbm, count_hbm, values_hbm, gain_hbm, out_hbm, start, count, values, gain, out, small, large, sent):
    devices, sites, width = out.shape
    span = width - gain.shape[1]
    wide, each = values.shape[1] // STEPS, devices // STEPS
    arriving = [
        pltpu.make_async_copy(start_hbm, start, small.at[0]),
        pltpu.make_async_copy(count_hbm, count, small.at[1]),
        pltpu.make_async_copy(gain_hbm, gain, small.at[2]),
    ]
    chunks = []
    for step in range(STEPS):
        part = (slice(None), pl.ds(step * wide, wide))
        chunks.append(pltpu.make_async_copy(values_hbm.at[part], values.at[part], large.at[step]))
    for copy in arriving + chunks:
        copy.start()
    for copy in arriving:
        copy.wait()
    site = lax.broadcasted_iota(jnp.int32, (sites, span), 0)
    first = end = jnp.zeros((sites, span), jnp.int32)
    for s in range(sites):
        first = jnp.where(site == s, start[s], first)
        end = jnp.where(site == s, start[s] + count[s], end)
    epoch = lax.broadcasted_iota(jnp.int32, (sites, span), 1)
    gains = gain[...]
    leaving = []
    for step in range(STEPS):
        chunks[step].wait()
        for to in range(step * each, (step + 1) * each):
            own = values[:, to * span:(to + 1) * span].astype(jnp.float32)
            inside = (epoch + to * span >= first) & (epoch + to * span < end)
            out[to, :, :span] = jnp.where(inside, own, 0.0).astype(out.dtype)
            out[to, :, span:] = gains
        part = pl.ds(step * each, each)
        leaving.append(pltpu.make_async_copy(out.at[part], out_hbm.at[part], sent.at[step]))
        leaving[-1].start()
    for copy in leaving:
        copy.wait()


def drive_kernel(got_ref, out_ref):
    sources, sites, width = got_ref.shape
    blocks, parts, slab, share = out_ref.shape
    span = parts * slab
    rows = got_ref[:, :, :span].reshape(sources * sites, span)
    gains = got_ref[:, :, span:].reshape(sources * sites, blocks * share)
    partial = lax.dot_general(rows, gains, (((0,), (0,)), ((), ())), preferred_element_type=jnp.float32)
    partial = partial.astype(out_ref.dtype)
    for block in range(blocks):
        for part in range(parts):
            out_ref[block, part] = partial[part * slab:(part + 1) * slab, block * share:(block + 1) * share]


def shifted(value, by, fill):
    count = value.shape[0]
    row = lax.broadcasted_iota(jnp.int32, value.shape, 0)
    moved = pltpu.roll(value, by % count, 0)
    inside = row >= by if by > 0 else row < count + by
    return jnp.where(inside, moved, fill)


def across(rate, states, sign):
    step = 1
    while step < ROWS:
        states = [s + rate * shifted(s, sign * step, 0.0) for s in states]
        rate = rate * shifted(rate, sign * step, 1.0)
        step *= 2
    return shifted(rate, sign, 1.0), [shifted(s, sign, 0.0) for s in states]


def scan_kernel(parts_ref, decay_ref, persist_ref, smooth_ref, entry_ref, product_ref, summary_ref, inj):
    sources, slab, width = parts_ref.shape
    total = parts_ref[0].astype(jnp.float32)
    for source in range(1, sources):
        total = total + parts_ref[source].astype(jnp.float32)
    inj[...] = jnp.sqrt(1.0 - decay_ref[...] * decay_ref[...]) * total
    depth = slab // ROWS
    persist = persist_ref[...]

    def rows(ref, j):
        return ref[pl.ds(j, ROWS, stride=depth), :]

    decays = [rows(decay_ref, j) for j in range(depth)]
    decayed, local = [decays[0]], [rows(inj, 0)]
    for j in range(1, depth):
        decayed.append(decays[j] * decayed[-1])
        local.append(decays[j] * local[-1] + rows(inj, j))
    enter_rate, (enter,) = across(decayed[-1], [local[-1]], 1)
    local = [h + a * enter for h, a in zip(local, decayed)]
    decayed = [a * enter_rate for a in decayed]
    products, smooth, entry = [None] * depth, [None] * depth, [None] * depth
    for j in reversed(range(depth)):
        rate = persist * decays[j]
        keep = 1.0 - rate * decays[j]
        if j == depth - 1:
            products[j], smooth[j], entry[j] = rate, keep * local[j], keep * decayed[j]
        else:
            products[j] = rate * products[j + 1]
            smooth[j] = rate * smooth[j + 1] + keep * local[j]
            entry[j] = rate * entry[j + 1] + keep * decayed[j]
    leave_rate, (leave_smooth, leave_entry) = across(products[0], [smooth[0], entry[0]], -1)
    for j in range(depth):
        smooth[j] = smooth[j] + products[j] * leave_smooth
        entry[j] = entry[j] + products[j] * leave_entry
        products[j] = products[j] * leave_rate
        smooth_ref[pl.ds(j, ROWS, stride=depth), :] = smooth[j]
        entry_ref[pl.ds(j, ROWS, stride=depth), :] = entry[j]
        product_ref[pl.ds(j, ROWS, stride=depth), :] = products[j]
    summary = [decayed[-1][ROWS - 1:], local[-1][ROWS - 1:], products[0][:1], smooth[0][:1], entry[0][:1]]
    summary = jnp.concatenate(summary + [jnp.zeros((3, width), jnp.float32)], axis=0)
    for to in range(summary_ref.shape[0]):
        summary_ref[to] = summary


def finish_kernel(place_ref, slabs_ref, smooth_ref, entry_ref, product_ref, rounded_ref, fwd, bwd):
    count, _, width = slabs_ref.shape

    def of(at, what):
        return slabs_ref[at, what:what + 1, :]

    state = jnp.zeros((1, width), jnp.float32)
    for at in range(count):
        fwd[at:at + 1, :] = state
        state = of(at, 0) * state + of(at, 1)
    state = jnp.zeros((1, width), jnp.float32)
    for at in reversed(range(count)):
        bwd[at:at + 1, :] = state
        state = of(at, 2) * state + (of(at, 3) + of(at, 4) * fwd[at:at + 1, :])
    place = place_ref[0]
    f_in, g_in = fwd[pl.ds(place, 1), :], bwd[pl.ds(place, 1), :]
    smoothed = smooth_ref[...] + entry_ref[...] * f_in + product_ref[...] * g_in
    rounded = smoothed.T.astype(rounded_ref.dtype)
    for to in range(rounded_ref.shape[0]):
        rounded_ref[to] = rounded


def predict_kernel(where_ref, near_ref, far_ref, mine_ref, pair_ref, out_ref):
    blocks, share, slab = mine_ref.shape
    pairs, _, sites, span = out_ref.shape
    first, core = where_ref[0] == 0, where_ref[1]
    mine, pair = mine_ref[...].reshape(blocks * share, slab), pair_ref[...].reshape(blocks * share, slab)
    states = jnp.concatenate([jnp.where(first, mine, pair), jnp.where(first, pair, mine)], axis=1)
    loadings = jnp.concatenate([near_ref[...], far_ref[...]], axis=0)
    predicted = jnp.dot(loadings, states, preferred_element_type=jnp.float32)
    predicted = predicted.astype(out_ref.dtype).reshape(2, pairs, sites, span)
    for other in range(2):
        out_ref[:, core ^ other] = predicted[other]


def call(kernel, name, out_shape, *args, scratch=(), scalars=0, vmem=32, **grid):
    if "in_specs" not in grid:
        specs = [pl.BlockSpec(memory_space=pltpu.SMEM)] * scalars
        specs += [pl.BlockSpec(memory_space=pltpu.VMEM)] * (len(args) - scalars)
        grid = dict(in_specs=specs)
    return pl.pallas_call(
        kernel,
        out_shape=out_shape,
        scratch_shapes=list(scratch),
        compiler_params=pltpu.CompilerParams(vmem_limit_bytes=vmem << 20),
        name=name,
        **grid,
    )(*args)


def per_device(observations, site_start, site_count, site_gain, site_loading, decay, persistence):
    planes, col, plane = ("zh", "zl"), ("y", "core"), ("x", "y", "core")
    line = plane + ("zl",)
    blocks, parts, nc = lax.axis_size("zh"), lax.axis_size("zl"), lax.axis_size(col)
    devices, slabs = lax.axis_size(plane), lax.axis_size(line)
    sites, epochs = observations.shape
    slab, span = epochs // slabs, epochs // devices
    basis = site_gain.shape[1]
    share = basis // blocks
    f32, bf16 = jnp.float32, jnp.bfloat16
    shape = jax.ShapeDtypeStruct
    turn = [
        ((h * parts + l) * nc + c, (c * parts + l) * nc + h)
        for h in range(blocks) for l in range(parts) for c in range(nc)
    ]

    hbm, smem = pl.BlockSpec(memory_space=pl.ANY), pltpu.SMEM
    sent = call(
        front_kernel, "front", shape((devices, sites, span + basis), bf16),
        site_start, site_count, observations, site_gain, in_specs=[hbm] * 4, out_specs=hbm, vmem=60,
        scratch=[
            smem((sites,), jnp.int32), smem((sites,), jnp.int32),
            pltpu.VMEM((sites, epochs), bf16), pltpu.VMEM((sites, basis), bf16),
            pltpu.VMEM((devices, sites, span + basis), bf16),
            pltpu.SemaphoreType.DMA((3,)), pltpu.SemaphoreType.DMA((STEPS,)), pltpu.SemaphoreType.DMA((STEPS,)),
        ],
    )
    got = lax.all_to_all(sent, plane, 0, 0, tiled=True)
    own = lax.dynamic_slice_in_dim(decay, lax.axis_index(col) * share, share, 1)
    decays = lax.ppermute(own, planes + col, turn)
    persist = lax.dynamic_slice_in_dim(persistence, lax.axis_index("zh") * share, share, 0)[None]
    got, decays, persist = lax.optimization_barrier((got, decays, persist))

    partial = call(drive_kernel, "drive", shape((blocks, parts, slab, share), bf16), got)
    summed = lax.all_to_all(partial.reshape(blocks * parts, slab, share), planes, 0, 0, tiled=True)
    near, _ = lax.optimization_barrier((site_loading, got))
    near = lax.all_gather(near, ("x", "y"), axis=0, tiled=True)
    summed, near = lax.optimization_barrier((summed, near))
    square = shape((slab, share), f32)
    smooth, entry, product, summary = call(
        scan_kernel, "scan", (square, square, square, shape((slabs, 8, share), f32)), summed, decays, persist,
        scratch=[pltpu.VMEM((slab, share), f32)],
    )
    summaries = lax.all_to_all(summary, line, 0, 0, tiled=True)
    far = lax.ppermute(near, "core", [(0, 1), (1, 0)])
    summaries, near, far = lax.optimization_barrier((summaries, near, far))
    rounded = call(
        finish_kernel, "finish", shape((blocks, share, slab), bf16),
        lax.axis_index(line).astype(jnp.int32)[None], summaries, smooth, entry, product,
        scratch=[pltpu.VMEM((slabs, share), f32)] * 2, scalars=1,
    )

    mine = lax.all_to_all(rounded, "zh", 0, 0, tiled=True)
    pair = lax.ppermute(mine, "zl", [(0, 1), (1, 0)])
    own = lax.all_to_all(mine, col, 0, 0, tiled=True)

    cores = lax.axis_size("core")
    where = jnp.stack([lax.axis_index("zl"), lax.axis_index("core")]).astype(jnp.int32)
    predicted = call(
        predict_kernel, "predict", shape((devices // cores, cores, sites, span), bf16),
        where, near, far, mine, pair, scalars=1,
    )
    predicted, own = lax.optimization_barrier((predicted, own))
    out = lax.dynamic_index_in_dim(own, lax.axis_index("zh"), 0, False).T.astype(f32)
    back = lax.all_to_all(predicted.reshape(devices, sites, span), plane, 0, 0, tiled=True)
    return (out, back.transpose(1, 0, 2).reshape(sites, epochs))


def solution(mesh):
    fine = Mesh(mesh.devices.reshape(4, 8, 2, 4, 2), ("x", "zh", "zl", "y", "core"))
    tm, col = ("x", "zh", "zl"), ("y", "core")
    every = tm + col
    return jax.shard_map(
        per_device,
        mesh=fine,
        in_specs=(P(every, None), P(every), P(every), P(every, None), P(every, None), P(tm, None), P()),
        out_specs=(P(tm, col), P(every, None)),
        check_vma=False,
    )
```

```python
import jax
import jax.numpy as jnp
from jax import lax
from jax.experimental import pallas as pl
from jax.experimental.pallas import tpu as pltpu
from jax.sharding import Mesh, PartitionSpec as P

ROWS = 8
STEPS = 4


def front_kernel(start_hbm, count_hbm, values_hbm, gain_hbm, out_hbm, start, count, values, gain, out, small, large, sent):
    devices, sites, width = out.shape
    span = width - gain.shape[1]
    wide, each = values.shape[1] // STEPS, devices // STEPS
    arriving = [
        pltpu.make_async_copy(start_hbm, start, small.at[0]),
        pltpu.make_async_copy(count_hbm, count, small.at[1]),
        pltpu.make_async_copy(gain_hbm, gain, small.at[2]),
    ]
    chunks = []
    for step in range(STEPS):
        part = (slice(None), pl.ds(step * wide, wide))
        chunks.append(pltpu.make_async_copy(values_hbm.at[part], values.at[part], large.at[step]))
    for copy in arriving + chunks:
        copy.start()
    for copy in arriving:
        copy.wait()
    site = lax.broadcasted_iota(jnp.int32, (sites, span), 0)
    first = end = jnp.zeros((sites, span), jnp.int32)
    for s in range(sites):
        first = jnp.where(site == s, start[s], first)
        end = jnp.where(site == s, start[s] + count[s], end)
    epoch = lax.broadcasted_iota(jnp.int32, (sites, span), 1)
    gains = gain[...]
    leaving = []
    for step in range(STEPS):
        chunks[step].wait()
        for to in range(step * each, (step + 1) * each):
            own = values[:, to * span:(to + 1) * span].astype(jnp.float32)
            inside = (epoch + to * span >= first) & (epoch + to * span < end)
            out[to, :, :span] = jnp.where(inside, own, 0.0).astype(out.dtype)
            out[to, :, span:] = gains
        part = pl.ds(step * each, each)
        leaving.append(pltpu.make_async_copy(out.at[part], out_hbm.at[part], sent.at[step]))
        leaving[-1].start()
    for copy in leaving:
        copy.wait()


def drive_kernel(got_ref, out_ref):
    sources, sites, width = got_ref.shape
    blocks, parts, slab, share = out_ref.shape
    span = parts * slab
    rows = got_ref[:, :, :span].reshape(sources * sites, span)
    gains = got_ref[:, :, span:].reshape(sources * sites, blocks * share)
    partial = lax.dot_general(rows, gains, (((0,), (0,)), ((), ())), preferred_element_type=jnp.float32)
    partial = partial.astype(out_ref.dtype)
    for block in range(blocks):
        for part in range(parts):
            out_ref[block, part] = partial[part * slab:(part + 1) * slab, block * share:(block + 1) * share]


def shifted(value, by, fill):
    count = value.shape[0]
    row = lax.broadcasted_iota(jnp.int32, value.shape, 0)
    moved = pltpu.roll(value, by % count, 0)
    inside = row >= by if by > 0 else row < count + by
    return jnp.where(inside, moved, fill)


def across(rate, states, sign):
    step = 1
    while step < ROWS:
        states = [s + rate * shifted(s, sign * step, 0.0) for s in states]
        rate = rate * shifted(rate, sign * step, 1.0)
        step *= 2
    return shifted(rate, sign, 1.0), [shifted(s, sign, 0.0) for s in states]


def scan_kernel(parts_ref, decay_ref, persist_ref, smooth_ref, entry_ref, product_ref, summary_ref, inj):
    sources, slab, width = parts_ref.shape
    total = parts_ref[0].astype(jnp.float32)
    for source in range(1, sources):
        total = total + parts_ref[source].astype(jnp.float32)
    inj[...] = jnp.sqrt(1.0 - decay_ref[...] * decay_ref[...]) * total
    depth = slab // ROWS
    persist = persist_ref[...]

    def rows(ref, j):
        return ref[pl.ds(j, ROWS, stride=depth), :]

    decays = [rows(decay_ref, j) for j in range(depth)]
    decayed, local = [decays[0]], [rows(inj, 0)]
    for j in range(1, depth):
        decayed.append(decays[j] * decayed[-1])
        local.append(decays[j] * local[-1] + rows(inj, j))
    enter_rate, (enter,) = across(decayed[-1], [local[-1]], 1)
    local = [h + a * enter for h, a in zip(local, decayed)]
    decayed = [a * enter_rate for a in decayed]
    products, smooth, entry = [None] * depth, [None] * depth, [None] * depth
    for j in reversed(range(depth)):
        rate = persist * decays[j]
        keep = 1.0 - rate * decays[j]
        if j == depth - 1:
            products[j], smooth[j], entry[j] = rate, keep * local[j], keep * decayed[j]
        else:
            products[j] = rate * products[j + 1]
            smooth[j] = rate * smooth[j + 1] + keep * local[j]
            entry[j] = rate * entry[j + 1] + keep * decayed[j]
    leave_rate, (leave_smooth, leave_entry) = across(products[0], [smooth[0], entry[0]], -1)
    for j in range(depth):
        smooth[j] = smooth[j] + products[j] * leave_smooth
        entry[j] = entry[j] + products[j] * leave_entry
        products[j] = products[j] * leave_rate
        smooth_ref[pl.ds(j, ROWS, stride=depth), :] = smooth[j]
        entry_ref[pl.ds(j, ROWS, stride=depth), :] = entry[j]
        product_ref[pl.ds(j, ROWS, stride=depth), :] = products[j]
    summary = [decayed[-1][ROWS - 1:], local[-1][ROWS - 1:], products[0][:1], smooth[0][:1], entry[0][:1]]
    summary = jnp.concatenate(summary + [jnp.zeros((3, width), jnp.float32)], axis=0)
    for to in range(summary_ref.shape[0]):
        summary_ref[to] = summary


def finish_kernel(place_ref, slabs_ref, smooth_ref, entry_ref, product_ref, rounded_ref, own_ref, fwd, bwd):
    count, _, width = slabs_ref.shape

    def of(at, what):
        return slabs_ref[at, what:what + 1, :]

    state = jnp.zeros((1, width), jnp.float32)
    for at in range(count):
        fwd[at:at + 1, :] = state
        state = of(at, 0) * state + of(at, 1)
    state = jnp.zeros((1, width), jnp.float32)
    for at in reversed(range(count)):
        bwd[at:at + 1, :] = state
        state = of(at, 2) * state + (of(at, 3) + of(at, 4) * fwd[at:at + 1, :])
    place = place_ref[0]
    f_in, g_in = fwd[pl.ds(place, 1), :], bwd[pl.ds(place, 1), :]
    smoothed = smooth_ref[...] + entry_ref[...] * f_in + product_ref[...] * g_in
    own_ref[...] = smoothed.astype(own_ref.dtype)
    rounded = smoothed.T.astype(rounded_ref.dtype)
    for to in range(rounded_ref.shape[0]):
        rounded_ref[to] = rounded


def predict_kernel(where_ref, near_ref, far_ref, pair_near_ref, pair_far_ref, states_ref, out_ref):
    blocks, share, slab = states_ref.shape
    chips, _, _, sites, _ = out_ref.shape
    core, part = where_ref[0], where_ref[1]
    states = states_ref[...].reshape(blocks * share, slab)
    for plane, refs in enumerate(((near_ref, far_ref), (pair_near_ref, pair_far_ref))):
        loadings = jnp.concatenate([ref[...] for ref in refs], axis=0)
        predicted = jnp.dot(loadings, states, preferred_element_type=jnp.float32)
        predicted = predicted.astype(out_ref.dtype).reshape(2, chips, sites, slab)
        for other in range(2):
            out_ref[:, core ^ other, part ^ plane] = predicted[other]


def call(kernel, name, out_shape, *args, scratch=(), scalars=0, vmem=32, **grid):
    if "in_specs" not in grid:
        specs = [pl.BlockSpec(memory_space=pltpu.SMEM)] * scalars
        specs += [pl.BlockSpec(memory_space=pltpu.VMEM)] * (len(args) - scalars)
        grid = dict(in_specs=specs)
    return pl.pallas_call(
        kernel,
        out_shape=out_shape,
        scratch_shapes=list(scratch),
        compiler_params=pltpu.CompilerParams(vmem_limit_bytes=vmem << 20),
        name=name,
        **grid,
    )(*args)


def per_device(observations, site_start, site_count, site_gain, site_loading, decay, persistence):
    planes, col, plane = ("zh", "zl"), ("y", "core"), ("x", "y", "core")
    line = plane + ("zl",)
    blocks, parts, nc = lax.axis_size("zh"), lax.axis_size("zl"), lax.axis_size(col)
    devices, slabs = lax.axis_size(plane), lax.axis_size(line)
    sites, epochs = observations.shape
    slab, span = epochs // slabs, epochs // devices
    basis = site_gain.shape[1]
    share = basis // blocks
    f32, bf16 = jnp.float32, jnp.bfloat16
    shape = jax.ShapeDtypeStruct
    turn = [
        ((h * parts + l) * nc + c, (c * parts + l) * nc + h)
        for h in range(blocks) for l in range(parts) for c in range(nc)
    ]

    hbm, smem = pl.BlockSpec(memory_space=pl.ANY), pltpu.SMEM
    sent = call(
        front_kernel, "front", shape((devices, sites, span + basis), bf16),
        site_start, site_count, observations, site_gain, in_specs=[hbm] * 4, out_specs=hbm, vmem=60,
        scratch=[
            smem((sites,), jnp.int32), smem((sites,), jnp.int32),
            pltpu.VMEM((sites, epochs), bf16), pltpu.VMEM((sites, basis), bf16),
            pltpu.VMEM((devices, sites, span + basis), bf16),
            pltpu.SemaphoreType.DMA((3,)), pltpu.SemaphoreType.DMA((STEPS,)), pltpu.SemaphoreType.DMA((STEPS,)),
        ],
    )
    got = lax.all_to_all(sent, plane, 0, 0, tiled=True)
    own = lax.dynamic_slice_in_dim(decay, lax.axis_index(col) * share, share, 1)
    decays = lax.ppermute(own, planes + col, turn)
    persist = lax.dynamic_slice_in_dim(persistence, lax.axis_index("zh") * share, share, 0)[None]
    got, decays, persist = lax.optimization_barrier((got, decays, persist))

    partial = call(drive_kernel, "drive", shape((blocks, parts, slab, share), bf16), got)
    summed = lax.all_to_all(partial.reshape(blocks * parts, slab, share), planes, 0, 0, tiled=True)
    near, _ = lax.optimization_barrier((site_loading, got))
    near = lax.all_gather(near, ("x", "y"), axis=0, tiled=True)
    swap = [(0, 1), (1, 0)]
    pair_near, far = lax.ppermute(near, "zl", swap), lax.ppermute(near, "core", swap)
    summed, near = lax.optimization_barrier((summed, near))
    square = shape((slab, share), f32)
    smooth, entry, product, summary = call(
        scan_kernel, "scan", (square, square, square, shape((slabs, 8, share), f32)), summed, decays, persist,
        scratch=[pltpu.VMEM((slab, share), f32)],
    )
    summaries = lax.all_to_all(summary, line, 0, 0, tiled=True)
    summaries, near, far, pair_near = lax.optimization_barrier((summaries, near, far, pair_near))
    rounded, own = call(
        finish_kernel, "finish", (shape((blocks, share, slab), bf16), shape((slab, share), bf16)),
        lax.axis_index(line).astype(jnp.int32)[None], summaries, smooth, entry, product,
        scratch=[pltpu.VMEM((slabs, share), f32)] * 2, scalars=1,
    )

    states = lax.all_to_all(rounded, "zh", 0, 0, tiled=True)
    pair_far = lax.ppermute(pair_near, "core", swap)
    out = lax.ppermute(own, planes + col, turn)
    states, pair_far, out = lax.optimization_barrier((states, pair_far, out))

    cores = lax.axis_size("core")
    where = jnp.stack([lax.axis_index("core"), lax.axis_index("zl")]).astype(jnp.int32)
    predicted = call(
        predict_kernel, "predict", shape((devices // cores, cores, parts, sites, slab), bf16),
        where, near, far, pair_near, pair_far, states, scalars=1,
    )
    back = lax.all_to_all(predicted.reshape(slabs, sites, slab), line, 0, 0, tiled=True)
    return (out.astype(f32), back.transpose(1, 0, 2).reshape(sites, epochs))


def solution(mesh):
    fine = Mesh(mesh.devices.reshape(4, 8, 2, 4, 2), ("x", "zh", "zl", "y", "core"))
    tm, col = ("x", "zh", "zl"), ("y", "core")
    every = tm + col
    return jax.shard_map(
        per_device,
        mesh=fine,
        in_specs=(P(every, None), P(every), P(every), P(every, None), P(every, None), P(tm, None), P()),
        out_specs=(P(tm, col), P(every, None)),
        check_vma=False,
    )
```

```python
import jax
import jax.numpy as jnp
from jax import lax
from jax.experimental import pallas as pl
from jax.experimental.pallas import tpu as pltpu
from jax.sharding import Mesh, PartitionSpec as P

ROWS = 8
STEPS = 4


def front_kernel(start_hbm, count_hbm, values_hbm, gain_hbm, out_hbm, start, count, values, gain, out, small, large, sent):
    devices, sites, width = out.shape
    span = width - gain.shape[1]
    wide, each = values.shape[1] // STEPS, devices // STEPS
    arriving = [
        pltpu.make_async_copy(start_hbm, start, small.at[0]),
        pltpu.make_async_copy(count_hbm, count, small.at[1]),
        pltpu.make_async_copy(gain_hbm, gain, small.at[2]),
    ]
    chunks = []
    for step in range(STEPS):
        part = (slice(None), pl.ds(step * wide, wide))
        chunks.append(pltpu.make_async_copy(values_hbm.at[part], values.at[part], large.at[step]))
    for copy in arriving + chunks:
        copy.start()
    for copy in arriving:
        copy.wait()
    site = lax.broadcasted_iota(jnp.int32, (sites, span), 0)
    first = end = jnp.zeros((sites, span), jnp.int32)
    for s in range(sites):
        first = jnp.where(site == s, start[s], first)
        end = jnp.where(site == s, start[s] + count[s], end)
    epoch = lax.broadcasted_iota(jnp.int32, (sites, span), 1)
    gains = gain[...]
    leaving = []
    for step in range(STEPS):
        chunks[step].wait()
        for to in range(step * each, (step + 1) * each):
            own = values[:, to * span:(to + 1) * span].astype(jnp.float32)
            inside = (epoch + to * span >= first) & (epoch + to * span < end)
            out[to, :, :span] = jnp.where(inside, own, 0.0).astype(out.dtype)
            out[to, :, span:] = gains
        part = pl.ds(step * each, each)
        leaving.append(pltpu.make_async_copy(out.at[part], out_hbm.at[part], sent.at[step]))
        leaving[-1].start()
    for copy in leaving:
        copy.wait()


def drive_kernel(part_ref, got_ref, keep_ref, give_ref):
    sources, sites, width = got_ref.shape
    blocks, slab, share = keep_ref.shape
    span = width - blocks * share
    rows = got_ref[:, :, :span].reshape(sources * sites, span)
    gains = got_ref[:, :, span:].reshape(sources * sites, blocks * share)
    partial = lax.dot_general(rows, gains, (((0,), (0,)), ((), ())), preferred_element_type=jnp.float32)
    first = part_ref[0] == 0
    keep = jnp.where(first, partial[:slab], partial[slab:])
    give = jnp.where(first, partial[slab:], partial[:slab]).astype(give_ref.dtype)
    for block in range(blocks):
        keep_ref[block] = keep[:, block * share:(block + 1) * share]
        give_ref[block] = give[:, block * share:(block + 1) * share]


def shifted(value, by, fill):
    count = value.shape[0]
    row = lax.broadcasted_iota(jnp.int32, value.shape, 0)
    moved = pltpu.roll(value, by % count, 0)
    inside = row >= by if by > 0 else row < count + by
    return jnp.where(inside, moved, fill)


def across(rate, states, sign):
    step = 1
    while step < ROWS:
        states = [s + rate * shifted(s, sign * step, 0.0) for s in states]
        rate = rate * shifted(rate, sign * step, 1.0)
        step *= 2
    return shifted(rate, sign, 1.0), [shifted(s, sign, 0.0) for s in states]


def scan_kernel(parts_ref, decay_ref, persist_ref, smooth_ref, entry_ref, product_ref, summary_ref, inj):
    sources, slab, width = parts_ref.shape
    total = parts_ref[0].astype(jnp.float32)
    for source in range(1, sources):
        total = total + parts_ref[source].astype(jnp.float32)
    inj[...] = jnp.sqrt(1.0 - decay_ref[...] * decay_ref[...]) * total
    depth = slab // ROWS
    persist = persist_ref[...]

    def rows(ref, j):
        return ref[pl.ds(j, ROWS, stride=depth), :]

    decays = [rows(decay_ref, j) for j in range(depth)]
    decayed, local = [decays[0]], [rows(inj, 0)]
    for j in range(1, depth):
        decayed.append(decays[j] * decayed[-1])
        local.append(decays[j] * local[-1] + rows(inj, j))
    enter_rate, (enter,) = across(decayed[-1], [local[-1]], 1)
    local = [h + a * enter for h, a in zip(local, decayed)]
    decayed = [a * enter_rate for a in decayed]
    products, smooth, entry = [None] * depth, [None] * depth, [None] * depth
    for j in reversed(range(depth)):
        rate = persist * decays[j]
        keep = 1.0 - rate * decays[j]
        if j == depth - 1:
            products[j], smooth[j], entry[j] = rate, keep * local[j], keep * decayed[j]
        else:
            products[j] = rate * products[j + 1]
            smooth[j] = rate * smooth[j + 1] + keep * local[j]
            entry[j] = rate * entry[j + 1] + keep * decayed[j]
    leave_rate, (leave_smooth, leave_entry) = across(products[0], [smooth[0], entry[0]], -1)
    for j in range(depth):
        smooth[j] = smooth[j] + products[j] * leave_smooth
        entry[j] = entry[j] + products[j] * leave_entry
        products[j] = products[j] * leave_rate
        smooth_ref[pl.ds(j, ROWS, stride=depth), :] = smooth[j]
        entry_ref[pl.ds(j, ROWS, stride=depth), :] = entry[j]
        product_ref[pl.ds(j, ROWS, stride=depth), :] = products[j]
    summary = [decayed[-1][ROWS - 1:], local[-1][ROWS - 1:], products[0][:1], smooth[0][:1], entry[0][:1]]
    summary = jnp.concatenate(summary + [jnp.zeros((3, width), jnp.float32)], axis=0)
    for to in range(summary_ref.shape[0]):
        summary_ref[to] = summary


def finish_kernel(place_ref, slabs_ref, smooth_ref, entry_ref, product_ref, rounded_ref, fwd, bwd):
    count, _, width = slabs_ref.shape

    def of(at, what):
        return slabs_ref[at, what:what + 1, :]

    state = jnp.zeros((1, width), jnp.float32)
    for at in range(count):
        fwd[at:at + 1, :] = state
        state = of(at, 0) * state + of(at, 1)
    state = jnp.zeros((1, width), jnp.float32)
    for at in reversed(range(count)):
        bwd[at:at + 1, :] = state
        state = of(at, 2) * state + (of(at, 3) + of(at, 4) * fwd[at:at + 1, :])
    place = place_ref[0]
    f_in, g_in = fwd[pl.ds(place, 1), :], bwd[pl.ds(place, 1), :]
    smoothed = smooth_ref[...] + entry_ref[...] * f_in + product_ref[...] * g_in
    rounded = smoothed.T.astype(rounded_ref.dtype)
    for to in range(rounded_ref.shape[0]):
        rounded_ref[to] = rounded


def predict_kernel(where_ref, near_ref, far_ref, mine_ref, pair_ref, out_ref):
    blocks, share, slab = mine_ref.shape
    nx, ny, cores, sites, span = out_ref.shape
    first, core, y = where_ref[0] == 0, where_ref[1], where_ref[2]
    mine, pair = mine_ref[...].reshape(blocks * share, slab), pair_ref[...].reshape(blocks * share, slab)
    states = jnp.concatenate([jnp.where(first, mine, pair), jnp.where(first, pair, mine)], axis=1)
    loadings = jnp.concatenate([near_ref[...], far_ref[...]], axis=0)
    predicted = jnp.dot(loadings, states, preferred_element_type=jnp.float32)
    predicted = predicted.astype(out_ref.dtype).reshape(cores, nx, ny, sites, span)
    for other in range(cores):
        for step in range(ny):
            out_ref[:, y ^ step, core ^ other] = predicted[other, :, step]


def call(kernel, name, out_shape, *args, scratch=(), scalars=0, vmem=32, **grid):
    if "in_specs" not in grid:
        specs = [pl.BlockSpec(memory_space=pltpu.SMEM)] * scalars
        specs += [pl.BlockSpec(memory_space=pltpu.VMEM)] * (len(args) - scalars)
        grid = dict(in_specs=specs)
    return pl.pallas_call(
        kernel,
        out_shape=out_shape,
        scratch_shapes=list(scratch),
        compiler_params=pltpu.CompilerParams(vmem_limit_bytes=vmem << 20),
        name=name,
        **grid,
    )(*args)


def per_device(observations, site_start, site_count, site_gain, site_loading, decay, persistence):
    planes, col, plane = ("zh", "zl"), ("y", "core"), ("x", "y", "core")
    line = plane + ("zl",)
    blocks, parts, nc = lax.axis_size("zh"), lax.axis_size("zl"), lax.axis_size(col)
    devices, slabs = lax.axis_size(plane), lax.axis_size(line)
    sites, epochs = observations.shape
    slab, span = epochs // slabs, epochs // devices
    basis = site_gain.shape[1]
    share = basis // blocks
    f32, bf16 = jnp.float32, jnp.bfloat16
    shape = jax.ShapeDtypeStruct
    turn = [
        ((h * parts + l) * nc + c, (c * parts + l) * nc + h)
        for h in range(blocks) for l in range(parts) for c in range(nc)
    ]

    hbm, smem = pl.BlockSpec(memory_space=pl.ANY), pltpu.SMEM
    sent = call(
        front_kernel, "front", shape((devices, sites, span + basis), bf16),
        site_start, site_count, observations, site_gain, in_specs=[hbm] * 4, out_specs=hbm, vmem=60,
        scratch=[
            smem((sites,), jnp.int32), smem((sites,), jnp.int32),
            pltpu.VMEM((sites, epochs), bf16), pltpu.VMEM((sites, basis), bf16),
            pltpu.VMEM((devices, sites, span + basis), bf16),
            pltpu.SemaphoreType.DMA((3,)), pltpu.SemaphoreType.DMA((STEPS,)), pltpu.SemaphoreType.DMA((STEPS,)),
        ],
    )
    got = lax.all_to_all(sent, plane, 0, 0, tiled=True)
    own = lax.dynamic_slice_in_dim(decay, lax.axis_index(col) * share, share, 1)
    decays = lax.ppermute(own, planes + col, turn)
    persist = lax.dynamic_slice_in_dim(persistence, lax.axis_index("zh") * share, share, 0)[None]
    ny, cores = lax.axis_size("y"), lax.axis_size("core")
    near = [site_loading]
    near += [lax.ppermute(site_loading, "y", [(i, i ^ step) for i in range(ny)]) for step in range(1, ny)]
    got, decays, persist, *near = lax.optimization_barrier((got, decays, persist, *near))

    part = lax.axis_index("zl").astype(jnp.int32)
    swap = [(0, 1), (1, 0)]
    both = (shape((blocks, slab, share), f32), shape((blocks, slab, share), bf16))
    keep, give = call(drive_kernel, "drive", both, part[None], got, scalars=1)
    taken, near = lax.optimization_barrier((lax.ppermute(give, "zl", swap), jnp.concatenate(near)))
    halves = (keep + taken.astype(f32)).astype(bf16)
    summed = lax.all_to_all(halves, "zh", 0, 0, tiled=True)
    near = lax.all_gather(near, "x", axis=0, tiled=True)
    summed, near = lax.optimization_barrier((summed, near))
    square = shape((slab, share), f32)
    smooth, entry, product, summary = call(
        scan_kernel, "scan", (square, square, square, shape((slabs, 8, share), f32)), summed, decays, persist,
        scratch=[pltpu.VMEM((slab, share), f32)],
    )
    summaries = lax.all_to_all(summary, line, 0, 0, tiled=True)
    far = lax.ppermute(near, "core", swap)
    summaries, near, far = lax.optimization_barrier((summaries, near, far))
    rounded = call(
        finish_kernel, "finish", shape((blocks, share, slab), bf16),
        lax.axis_index(line).astype(jnp.int32)[None], summaries, smooth, entry, product,
        scratch=[pltpu.VMEM((slabs, share), f32)] * 2, scalars=1,
    )

    mine = lax.all_to_all(rounded, "zh", 0, 0, tiled=True)
    pair = lax.ppermute(mine, "zl", swap)
    own = lax.all_to_all(mine, col, 0, 0, tiled=True)

    where = jnp.stack([part, lax.axis_index("core").astype(jnp.int32), lax.axis_index("y").astype(jnp.int32)])
    predicted = call(
        predict_kernel, "predict", shape((devices // cores // ny, ny, cores, sites, span), bf16),
        where, near, far, mine, pair, scalars=1,
    )
    predicted, own = lax.optimization_barrier((predicted, own))
    out = lax.dynamic_index_in_dim(own, lax.axis_index("zh"), 0, False).T.astype(f32)
    back = lax.all_to_all(predicted.reshape(devices, sites, span), plane, 0, 0, tiled=True)
    return (out, back.transpose(1, 0, 2).reshape(sites, epochs))


def solution(mesh):
    fine = Mesh(mesh.devices.reshape(4, 8, 2, 4, 2), ("x", "zh", "zl", "y", "core"))
    tm, col = ("x", "zh", "zl"), ("y", "core")
    every = tm + col
    return jax.shard_map(
        per_device,
        mesh=fine,
        in_specs=(P(every, None), P(every), P(every), P(every, None), P(every, None), P(tm, None), P()),
        out_specs=(P(tm, col), P(every, None)),
        check_vma=False,
    )
```

```python
import jax
import jax.numpy as jnp
from jax import lax
from jax.experimental import pallas as pl
from jax.experimental.pallas import tpu as pltpu
from jax.sharding import Mesh, PartitionSpec as P

ROWS = 8
STEPS = 4


def front_kernel(start_hbm, count_hbm, values_hbm, gain_hbm, out_hbm, start, count, values, gain, out, small, large, sent):
    devices, sites, width = out.shape
    span = width - gain.shape[1]
    wide, each = values.shape[1] // STEPS, devices // STEPS
    arriving = [
        pltpu.make_async_copy(start_hbm, start, small.at[0]),
        pltpu.make_async_copy(count_hbm, count, small.at[1]),
        pltpu.make_async_copy(gain_hbm, gain, small.at[2]),
    ]
    chunks = []
    for step in range(STEPS):
        part = (slice(None), pl.ds(step * wide, wide))
        chunks.append(pltpu.make_async_copy(values_hbm.at[part], values.at[part], large.at[step]))
    for copy in arriving + chunks:
        copy.start()
    for copy in arriving:
        copy.wait()
    site = lax.broadcasted_iota(jnp.int32, (sites, span), 0)
    first = end = jnp.zeros((sites, span), jnp.int32)
    for s in range(sites):
        first = jnp.where(site == s, start[s], first)
        end = jnp.where(site == s, start[s] + count[s], end)
    epoch = lax.broadcasted_iota(jnp.int32, (sites, span), 1)
    gains = gain[...]
    leaving = []
    for step in range(STEPS):
        chunks[step].wait()
        for to in range(step * each, (step + 1) * each):
            own = values[:, to * span:(to + 1) * span].astype(jnp.float32)
            inside = (epoch + to * span >= first) & (epoch + to * span < end)
            out[to, :, :span] = jnp.where(inside, own, 0.0).astype(out.dtype)
            out[to, :, span:] = gains
        part = pl.ds(step * each, each)
        leaving.append(pltpu.make_async_copy(out.at[part], out_hbm.at[part], sent.at[step]))
        leaving[-1].start()
    for copy in leaving:
        copy.wait()


def drive_kernel(part_ref, got_ref, keep_ref, give_ref):
    sources, sites, width = got_ref.shape
    blocks, slab, share = keep_ref.shape
    span = width - blocks * share
    rows = got_ref[:, :, :span].reshape(sources * sites, span)
    gains = got_ref[:, :, span:].reshape(sources * sites, blocks * share)
    partial = lax.dot_general(rows, gains, (((0,), (0,)), ((), ())), preferred_element_type=jnp.float32)
    first = part_ref[0] == 0
    keep = jnp.where(first, partial[:slab], partial[slab:])
    give = jnp.where(first, partial[slab:], partial[:slab]).astype(give_ref.dtype)
    for block in range(blocks):
        keep_ref[block] = keep[:, block * share:(block + 1) * share]
        give_ref[block] = give[:, block * share:(block + 1) * share]


def shifted(value, by, fill):
    count = value.shape[0]
    row = lax.broadcasted_iota(jnp.int32, value.shape, 0)
    moved = pltpu.roll(value, by % count, 0)
    inside = row >= by if by > 0 else row < count + by
    return jnp.where(inside, moved, fill)


def across(rate, states, sign):
    step = 1
    while step < ROWS:
        states = [s + rate * shifted(s, sign * step, 0.0) for s in states]
        rate = rate * shifted(rate, sign * step, 1.0)
        step *= 2
    return shifted(rate, sign, 1.0), [shifted(s, sign, 0.0) for s in states]


def scan_kernel(parts_ref, decay_ref, persist_ref, smooth_ref, entry_ref, product_ref, summary_ref, inj):
    sources, slab, width = parts_ref.shape
    total = parts_ref[0].astype(jnp.float32)
    for source in range(1, sources):
        total = total + parts_ref[source].astype(jnp.float32)
    inj[...] = jnp.sqrt(1.0 - decay_ref[...] * decay_ref[...]) * total
    depth = slab // ROWS
    persist = persist_ref[...]

    def rows(ref, j):
        return ref[pl.ds(j, ROWS, stride=depth), :]

    decays = [rows(decay_ref, j) for j in range(depth)]
    decayed, local = [decays[0]], [rows(inj, 0)]
    for j in range(1, depth):
        decayed.append(decays[j] * decayed[-1])
        local.append(decays[j] * local[-1] + rows(inj, j))
    enter_rate, (enter,) = across(decayed[-1], [local[-1]], 1)
    local = [h + a * enter for h, a in zip(local, decayed)]
    decayed = [a * enter_rate for a in decayed]
    products, smooth, entry = [None] * depth, [None] * depth, [None] * depth
    for j in reversed(range(depth)):
        rate = persist * decays[j]
        keep = 1.0 - rate * decays[j]
        if j == depth - 1:
            products[j], smooth[j], entry[j] = rate, keep * local[j], keep * decayed[j]
        else:
            products[j] = rate * products[j + 1]
            smooth[j] = rate * smooth[j + 1] + keep * local[j]
            entry[j] = rate * entry[j + 1] + keep * decayed[j]
    leave_rate, (leave_smooth, leave_entry) = across(products[0], [smooth[0], entry[0]], -1)
    for j in range(depth):
        smooth[j] = smooth[j] + products[j] * leave_smooth
        entry[j] = entry[j] + products[j] * leave_entry
        products[j] = products[j] * leave_rate
        smooth_ref[pl.ds(j, ROWS, stride=depth), :] = smooth[j]
        entry_ref[pl.ds(j, ROWS, stride=depth), :] = entry[j]
        product_ref[pl.ds(j, ROWS, stride=depth), :] = products[j]
    summary = [decayed[-1][ROWS - 1:], local[-1][ROWS - 1:], products[0][:1], smooth[0][:1], entry[0][:1]]
    summary = jnp.concatenate(summary + [jnp.zeros((3, width), jnp.float32)], axis=0)
    for to in range(summary_ref.shape[0]):
        summary_ref[to] = summary


def finish_kernel(place_ref, slabs_ref, smooth_ref, entry_ref, product_ref, rounded_ref, fwd, bwd):
    count, _, width = slabs_ref.shape

    def of(at, what):
        return slabs_ref[at, what:what + 1, :]

    state = jnp.zeros((1, width), jnp.float32)
    for at in range(count):
        fwd[at:at + 1, :] = state
        state = of(at, 0) * state + of(at, 1)
    state = jnp.zeros((1, width), jnp.float32)
    for at in reversed(range(count)):
        bwd[at:at + 1, :] = state
        state = of(at, 2) * state + (of(at, 3) + of(at, 4) * fwd[at:at + 1, :])
    place = place_ref[0]
    f_in, g_in = fwd[pl.ds(place, 1), :], bwd[pl.ds(place, 1), :]
    smoothed = smooth_ref[...] + entry_ref[...] * f_in + product_ref[...] * g_in
    rounded = smoothed.T.astype(rounded_ref.dtype)
    for to in range(rounded_ref.shape[0]):
        rounded_ref[to] = rounded


def predict_kernel(where_ref, near_ref, far_ref, mine_ref, pair_ref, out_ref):
    blocks, share, slab = mine_ref.shape
    nx, ny, cores, sites, span = out_ref.shape
    first, core, y = where_ref[0] == 0, where_ref[1], where_ref[2]
    mine, pair = mine_ref[...].reshape(blocks * share, slab), pair_ref[...].reshape(blocks * share, slab)
    states = jnp.concatenate([jnp.where(first, mine, pair), jnp.where(first, pair, mine)], axis=1)
    for other, ref in enumerate((near_ref, far_ref)):
        predicted = jnp.dot(ref[...], states, preferred_element_type=jnp.float32)
        predicted = predicted.astype(out_ref.dtype).reshape(ny, nx, sites, span)
        for step in range(ny):
            out_ref[:, y ^ step, core ^ other] = predicted[step]


def call(kernel, name, out_shape, *args, scratch=(), scalars=0, vmem=32, **grid):
    if "in_specs" not in grid:
        specs = [pl.BlockSpec(memory_space=pltpu.SMEM)] * scalars
        specs += [pl.BlockSpec(memory_space=pltpu.VMEM)] * (len(args) - scalars)
        grid = dict(in_specs=specs)
    return pl.pallas_call(
        kernel,
        out_shape=out_shape,
        scratch_shapes=list(scratch),
        compiler_params=pltpu.CompilerParams(vmem_limit_bytes=vmem << 20),
        name=name,
        **grid,
    )(*args)


def per_device(observations, site_start, site_count, site_gain, site_loading, decay, persistence):
    planes, col, plane = ("zh", "zl"), ("y", "core"), ("x", "y", "core")
    line = plane + ("zl",)
    blocks, parts, nc = lax.axis_size("zh"), lax.axis_size("zl"), lax.axis_size(col)
    devices, slabs = lax.axis_size(plane), lax.axis_size(line)
    sites, epochs = observations.shape
    slab, span = epochs // slabs, epochs // devices
    basis = site_gain.shape[1]
    share = basis // blocks
    f32, bf16 = jnp.float32, jnp.bfloat16
    shape = jax.ShapeDtypeStruct
    turn = [
        ((h * parts + l) * nc + c, (c * parts + l) * nc + h)
        for h in range(blocks) for l in range(parts) for c in range(nc)
    ]

    hbm, smem = pl.BlockSpec(memory_space=pl.ANY), pltpu.SMEM
    sent = call(
        front_kernel, "front", shape((devices, sites, span + basis), bf16),
        site_start, site_count, observations, site_gain, in_specs=[hbm] * 4, out_specs=hbm, vmem=60,
        scratch=[
            smem((sites,), jnp.int32), smem((sites,), jnp.int32),
            pltpu.VMEM((sites, epochs), bf16), pltpu.VMEM((sites, basis), bf16),
            pltpu.VMEM((devices, sites, span + basis), bf16),
            pltpu.SemaphoreType.DMA((3,)), pltpu.SemaphoreType.DMA((STEPS,)), pltpu.SemaphoreType.DMA((STEPS,)),
        ],
    )
    got = lax.all_to_all(sent, plane, 0, 0, tiled=True)
    own = lax.dynamic_slice_in_dim(decay, lax.axis_index(col) * share, share, 1)
    decays = lax.ppermute(own, planes + col, turn)
    persist = lax.dynamic_slice_in_dim(persistence, lax.axis_index("zh") * share, share, 0)[None]
    got, decays, persist = lax.optimization_barrier((got, decays, persist))

    part = lax.axis_index("zl").astype(jnp.int32)
    swap = [(0, 1), (1, 0)]
    both = (shape((blocks, slab, share), f32), shape((blocks, slab, share), bf16))
    keep, give = call(drive_kernel, "drive", both, part[None], got, scalars=1)
    taken, near = lax.optimization_barrier((lax.ppermute(give, "zl", swap), site_loading))
    halves = (keep + taken.astype(f32)).astype(bf16)
    summed = lax.all_to_all(halves, "zh", 0, 0, tiled=True)
    near = lax.all_gather(near, "x", axis=0, tiled=True)
    summed, near = lax.optimization_barrier((summed, near))
    square = shape((slab, share), f32)
    smooth, entry, product, summary = call(
        scan_kernel, "scan", (square, square, square, shape((slabs, 8, share), f32)), summed, decays, persist,
        scratch=[pltpu.VMEM((slab, share), f32)],
    )
    summaries = lax.all_to_all(summary, line, 0, 0, tiled=True)
    ny, cores = lax.axis_size("y"), lax.axis_size("core")
    near = [near] + [lax.ppermute(near, "y", [(i, i ^ step) for i in range(ny)]) for step in range(1, ny)]
    summaries, *near = lax.optimization_barrier((summaries, *near))
    rounded = call(
        finish_kernel, "finish", shape((blocks, share, slab), bf16),
        lax.axis_index(line).astype(jnp.int32)[None], summaries, smooth, entry, product,
        scratch=[pltpu.VMEM((slabs, share), f32)] * 2, scalars=1,
    )

    mine = lax.all_to_all(rounded, "zh", 0, 0, tiled=True)
    near = jnp.concatenate(near)
    mine, near, far = lax.optimization_barrier((mine, near, lax.ppermute(near, "core", swap)))
    pair = lax.ppermute(mine, "zl", swap)
    own = lax.all_to_all(mine, col, 0, 0, tiled=True)

    where = jnp.stack([part, lax.axis_index("core").astype(jnp.int32), lax.axis_index("y").astype(jnp.int32)])
    predicted = call(
        predict_kernel, "predict", shape((devices // cores // ny, ny, cores, sites, span), bf16),
        where, near, far, mine, pair, scalars=1,
    )
    predicted, own = lax.optimization_barrier((predicted, own))
    out = lax.dynamic_index_in_dim(own, lax.axis_index("zh"), 0, False).T.astype(f32)
    back = lax.all_to_all(predicted.reshape(devices, sites, span), plane, 0, 0, tiled=True)
    return (out, back.transpose(1, 0, 2).reshape(sites, epochs))


def solution(mesh):
    fine = Mesh(mesh.devices.reshape(4, 8, 2, 4, 2), ("x", "zh", "zl", "y", "core"))
    tm, col = ("x", "zh", "zl"), ("y", "core")
    every = tm + col
    return jax.shard_map(
        per_device,
        mesh=fine,
        in_specs=(P(every, None), P(every), P(every), P(every, None), P(every, None), P(tm, None), P()),
        out_specs=(P(tm, col), P(every, None)),
        check_vma=False,
    )
```

```python
import jax
import jax.numpy as jnp
from jax import lax
from jax.experimental import pallas as pl
from jax.experimental.pallas import tpu as pltpu
from jax.sharding import Mesh, PartitionSpec as P

ROWS = 8
STEPS = 4


def front_kernel(start_hbm, count_hbm, values_hbm, gain_hbm, out_hbm, start, count, values, gain, out, small, large, sent):
    devices, sites, width = out.shape
    half = gain.shape[1] // 2
    span = width - half
    wide, each = values.shape[1] // STEPS, devices // STEPS
    arriving = [
        pltpu.make_async_copy(start_hbm, start, small.at[0]),
        pltpu.make_async_copy(count_hbm, count, small.at[1]),
        pltpu.make_async_copy(gain_hbm, gain, small.at[2]),
    ]
    chunks = []
    for step in range(STEPS):
        part = (slice(None), pl.ds(step * wide, wide))
        chunks.append(pltpu.make_async_copy(values_hbm.at[part], values.at[part], large.at[step]))
    for copy in arriving + chunks:
        copy.start()
    for copy in arriving:
        copy.wait()
    site = lax.broadcasted_iota(jnp.int32, (sites, span), 0)
    first = end = jnp.zeros((sites, span), jnp.int32)
    for s in range(sites):
        first = jnp.where(site == s, start[s], first)
        end = jnp.where(site == s, start[s] + count[s], end)
    epoch = lax.broadcasted_iota(jnp.int32, (sites, span), 1)
    gains = gain[...]
    leaving = []
    for step in range(STEPS):
        chunks[step].wait()
        for to in range(step * each, (step + 1) * each):
            own = values[:, to * span:(to + 1) * span].astype(jnp.float32)
            inside = (epoch + to * span >= first) & (epoch + to * span < end)
            out[to, :, :span] = jnp.where(inside, own, 0.0).astype(out.dtype)
            out[to, :, span:] = gains[:, to % 2 * half:(to % 2 + 1) * half]
        part = pl.ds(step * each, each)
        leaving.append(pltpu.make_async_copy(out.at[part], out_hbm.at[part], sent.at[step]))
        leaving[-1].start()
    for copy in leaving:
        copy.wait()


def drive_kernel(core_ref, got_ref, other_ref, out_ref):
    sources, sites, half = other_ref.shape
    blocks, parts, slab, share = out_ref.shape
    span = parts * slab
    rows = got_ref[:, :, :span].reshape(sources * sites, span)
    for turn in range(2):
        gains = (got_ref[:, :, span:] if turn == 0 else other_ref[...]).reshape(sources * sites, half)
        partial = lax.dot_general(rows, gains, (((0,), (0,)), ((), ())), preferred_element_type=jnp.float32)
        partial = partial.astype(out_ref.dtype)
        first = (core_ref[0] ^ turn) * (blocks // 2)
        for block in range(blocks // 2):
            for part in range(parts):
                out_ref[first + block, part] = partial[part * slab:(part + 1) * slab, block * share:(block + 1) * share]


def shifted(value, by, fill):
    count = value.shape[0]
    row = lax.broadcasted_iota(jnp.int32, value.shape, 0)
    moved = pltpu.roll(value, by % count, 0)
    inside = row >= by if by > 0 else row < count + by
    return jnp.where(inside, moved, fill)


def across(rate, states, sign):
    step = 1
    while step < ROWS:
        states = [s + rate * shifted(s, sign * step, 0.0) for s in states]
        rate = rate * shifted(rate, sign * step, 1.0)
        step *= 2
    return shifted(rate, sign, 1.0), [shifted(s, sign, 0.0) for s in states]


def scan_kernel(parts_ref, decay_ref, persist_ref, smooth_ref, entry_ref, product_ref, summary_ref, inj):
    sources, slab, width = parts_ref.shape
    total = parts_ref[0].astype(jnp.float32)
    for source in range(1, sources):
        total = total + parts_ref[source].astype(jnp.float32)
    inj[...] = jnp.sqrt(1.0 - decay_ref[...] * decay_ref[...]) * total
    depth = slab // ROWS
    persist = persist_ref[...]

    def rows(ref, j):
        return ref[pl.ds(j, ROWS, stride=depth), :]

    decays = [rows(decay_ref, j) for j in range(depth)]
    decayed, local = [decays[0]], [rows(inj, 0)]
    for j in range(1, depth):
        decayed.append(decays[j] * decayed[-1])
        local.append(decays[j] * local[-1] + rows(inj, j))
    enter_rate, (enter,) = across(decayed[-1], [local[-1]], 1)
    local = [h + a * enter for h, a in zip(local, decayed)]
    decayed = [a * enter_rate for a in decayed]
    products, smooth, entry = [None] * depth, [None] * depth, [None] * depth
    for j in reversed(range(depth)):
        rate = persist * decays[j]
        keep = 1.0 - rate * decays[j]
        if j == depth - 1:
            products[j], smooth[j], entry[j] = rate, keep * local[j], keep * decayed[j]
        else:
            products[j] = rate * products[j + 1]
            smooth[j] = rate * smooth[j + 1] + keep * local[j]
            entry[j] = rate * entry[j + 1] + keep * decayed[j]
    leave_rate, (leave_smooth, leave_entry) = across(products[0], [smooth[0], entry[0]], -1)
    for j in range(depth):
        smooth[j] = smooth[j] + products[j] * leave_smooth
        entry[j] = entry[j] + products[j] * leave_entry
        products[j] = products[j] * leave_rate
        smooth_ref[pl.ds(j, ROWS, stride=depth), :] = smooth[j]
        entry_ref[pl.ds(j, ROWS, stride=depth), :] = entry[j]
        product_ref[pl.ds(j, ROWS, stride=depth), :] = products[j]
    summary = [decayed[-1][ROWS - 1:], local[-1][ROWS - 1:], products[0][:1], smooth[0][:1], entry[0][:1]]
    summary = jnp.concatenate(summary + [jnp.zeros((3, width), jnp.float32)], axis=0)
    for to in range(summary_ref.shape[0]):
        summary_ref[to] = summary


def finish_kernel(place_ref, slabs_ref, smooth_ref, entry_ref, product_ref, rounded_ref, fwd, bwd):
    count, _, width = slabs_ref.shape

    def of(at, what):
        return slabs_ref[at, what:what + 1, :]

    state = jnp.zeros((1, width), jnp.float32)
    for at in range(count):
        fwd[at:at + 1, :] = state
        state = of(at, 0) * state + of(at, 1)
    state = jnp.zeros((1, width), jnp.float32)
    for at in reversed(range(count)):
        bwd[at:at + 1, :] = state
        state = of(at, 2) * state + (of(at, 3) + of(at, 4) * fwd[at:at + 1, :])
    place = place_ref[0]
    f_in, g_in = fwd[pl.ds(place, 1), :], bwd[pl.ds(place, 1), :]
    smoothed = smooth_ref[...] + entry_ref[...] * f_in + product_ref[...] * g_in
    rounded = smoothed.T.astype(rounded_ref.dtype)
    for to in range(rounded_ref.shape[0]):
        rounded_ref[to] = rounded


def predict_kernel(where_ref, near_ref, far_ref, mine_ref, pair_ref, out_ref):
    blocks, share, slab = mine_ref.shape
    pairs, _, sites, span = out_ref.shape
    first, core = where_ref[0] == 0, where_ref[1]
    mine, pair = mine_ref[...].reshape(blocks * share, slab), pair_ref[...].reshape(blocks * share, slab)
    states = jnp.concatenate([jnp.where(first, mine, pair), jnp.where(first, pair, mine)], axis=1)
    loadings = jnp.concatenate([near_ref[...], far_ref[...]], axis=0)
    predicted = jnp.dot(loadings, states, preferred_element_type=jnp.float32)
    predicted = predicted.astype(out_ref.dtype).reshape(2, pairs, sites, span)
    for other in range(2):
        out_ref[:, core ^ other] = predicted[other]


def call(kernel, name, out_shape, *args, scratch=(), scalars=0, vmem=32, **grid):
    if "in_specs" not in grid:
        specs = [pl.BlockSpec(memory_space=pltpu.SMEM)] * scalars
        specs += [pl.BlockSpec(memory_space=pltpu.VMEM)] * (len(args) - scalars)
        grid = dict(in_specs=specs)
    return pl.pallas_call(
        kernel,
        out_shape=out_shape,
        scratch_shapes=list(scratch),
        compiler_params=pltpu.CompilerParams(vmem_limit_bytes=vmem << 20),
        name=name,
        **grid,
    )(*args)


def per_device(observations, site_start, site_count, site_gain, site_loading, decay, persistence):
    planes, col, plane = ("zh", "zl"), ("y", "core"), ("x", "y", "core")
    line = plane + ("zl",)
    blocks, parts, nc = lax.axis_size("zh"), lax.axis_size("zl"), lax.axis_size(col)
    devices, slabs = lax.axis_size(plane), lax.axis_size(line)
    sites, epochs = observations.shape
    slab, span = epochs // slabs, epochs // devices
    basis = site_gain.shape[1]
    share = basis // blocks
    f32, bf16 = jnp.float32, jnp.bfloat16
    shape = jax.ShapeDtypeStruct
    turn = [
        ((h * parts + l) * nc + c, (c * parts + l) * nc + h)
        for h in range(blocks) for l in range(parts) for c in range(nc)
    ]

    hbm, smem = pl.BlockSpec(memory_space=pl.ANY), pltpu.SMEM
    sent = call(
        front_kernel, "front", shape((devices, sites, span + basis // 2), bf16),
        site_start, site_count, observations, site_gain, in_specs=[hbm] * 4, out_specs=hbm, vmem=60,
        scratch=[
            smem((sites,), jnp.int32), smem((sites,), jnp.int32),
            pltpu.VMEM((sites, epochs), bf16), pltpu.VMEM((sites, basis), bf16),
            pltpu.VMEM((devices, sites, span + basis // 2), bf16),
            pltpu.SemaphoreType.DMA((3,)), pltpu.SemaphoreType.DMA((STEPS,)), pltpu.SemaphoreType.DMA((STEPS,)),
        ],
    )
    got = lax.all_to_all(sent, plane, 0, 0, tiled=True)
    own = lax.dynamic_slice_in_dim(decay, lax.axis_index(col) * share, share, 1)
    decays = lax.ppermute(own, planes + col, turn)
    persist = lax.dynamic_slice_in_dim(persistence, lax.axis_index("zh") * share, share, 0)[None]
    got, decays, persist = lax.optimization_barrier((got, decays, persist))

    swap = [(0, 1), (1, 0)]
    other = lax.ppermute(got[:, :, span:], "core", swap)
    core = lax.axis_index("core").astype(jnp.int32)
    partial = call(drive_kernel, "drive", shape((blocks, parts, slab, share), bf16), core[None], got, other, scalars=1)
    summed = lax.all_to_all(partial.reshape(blocks * parts, slab, share), planes, 0, 0, tiled=True)
    near, _ = lax.optimization_barrier((site_loading, other))
    near = lax.all_gather(near, ("x", "y"), axis=0, tiled=True)
    summed, near = lax.optimization_barrier((summed, near))
    square = shape((slab, share), f32)
    smooth, entry, product, summary = call(
        scan_kernel, "scan", (square, square, square, shape((slabs, 8, share), f32)), summed, decays, persist,
        scratch=[pltpu.VMEM((slab, share), f32)],
    )
    summaries = lax.all_to_all(summary, line, 0, 0, tiled=True)
    far = lax.ppermute(near, "core", [(0, 1), (1, 0)])
    summaries, near, far = lax.optimization_barrier((summaries, near, far))
    rounded = call(
        finish_kernel, "finish", shape((blocks, share, slab), bf16),
        lax.axis_index(line).astype(jnp.int32)[None], summaries, smooth, entry, product,
        scratch=[pltpu.VMEM((slabs, share), f32)] * 2, scalars=1,
    )

    mine = lax.all_to_all(rounded, "zh", 0, 0, tiled=True)
    pair = lax.ppermute(mine, "zl", [(0, 1), (1, 0)])
    own = lax.all_to_all(mine, col, 0, 0, tiled=True)

    cores = lax.axis_size("core")
    where = jnp.stack([lax.axis_index("zl"), lax.axis_index("core")]).astype(jnp.int32)
    predicted = call(
        predict_kernel, "predict", shape((devices // cores, cores, sites, span), bf16),
        where, near, far, mine, pair, scalars=1,
    )
    predicted, own = lax.optimization_barrier((predicted, own))
    out = lax.dynamic_index_in_dim(own, lax.axis_index("zh"), 0, False).T.astype(f32)
    back = lax.all_to_all(predicted.reshape(devices, sites, span), plane, 0, 0, tiled=True)
    return (out, back.transpose(1, 0, 2).reshape(sites, epochs))


def solution(mesh):
    fine = Mesh(mesh.devices.reshape(4, 8, 2, 4, 2), ("x", "zh", "zl", "y", "core"))
    tm, col = ("x", "zh", "zl"), ("y", "core")
    every = tm + col
    return jax.shard_map(
        per_device,
        mesh=fine,
        in_specs=(P(every, None), P(every), P(every), P(every, None), P(every, None), P(tm, None), P()),
        out_specs=(P(tm, col), P(every, None)),
        check_vma=False,
    )
```

```python
import jax
import jax.numpy as jnp
from jax import lax
from jax.experimental import pallas as pl
from jax.experimental.pallas import tpu as pltpu
from jax.sharding import Mesh, PartitionSpec as P

ROWS = 8
STEPS = 4


def front_kernel(start_hbm, count_hbm, values_hbm, gain_hbm, out_hbm, start, count, values, gain, out, small, large, sent):
    devices, sites, width = out.shape
    half = gain.shape[1] // 2
    span = width - half
    wide, each = values.shape[1] // STEPS, devices // STEPS
    arriving = [
        pltpu.make_async_copy(start_hbm, start, small.at[0]),
        pltpu.make_async_copy(count_hbm, count, small.at[1]),
        pltpu.make_async_copy(gain_hbm, gain, small.at[2]),
    ]
    chunks = []
    for step in range(STEPS):
        part = (slice(None), pl.ds(step * wide, wide))
        chunks.append(pltpu.make_async_copy(values_hbm.at[part], values.at[part], large.at[step]))
    for copy in arriving + chunks:
        copy.start()
    for copy in arriving:
        copy.wait()
    site = lax.broadcasted_iota(jnp.int32, (sites, span), 0)
    first = end = jnp.zeros((sites, span), jnp.int32)
    for s in range(sites):
        first = jnp.where(site == s, start[s], first)
        end = jnp.where(site == s, start[s] + count[s], end)
    epoch = lax.broadcasted_iota(jnp.int32, (sites, span), 1)
    gains = gain[...]
    leaving = []
    for step in range(STEPS):
        chunks[step].wait()
        for to in range(step * each, (step + 1) * each):
            own = values[:, to * span:(to + 1) * span].astype(jnp.float32)
            inside = (epoch + to * span >= first) & (epoch + to * span < end)
            out[to, :, :span] = jnp.where(inside, own, 0.0).astype(out.dtype)
            out[to, :, span:] = gains[:, to % 2 * half:(to % 2 + 1) * half]
        part = pl.ds(step * each, each)
        leaving.append(pltpu.make_async_copy(out.at[part], out_hbm.at[part], sent.at[step]))
        leaving[-1].start()
    for copy in leaving:
        copy.wait()


def drive_kernel(core_ref, got_ref, other_ref, out_ref):
    sources, sites, half = other_ref.shape
    blocks, parts, slab, share = out_ref.shape
    span = parts * slab
    rows = got_ref[:, :, :span].reshape(sources * sites, span)
    for turn in range(2):
        gains = (got_ref[:, :, span:] if turn == 0 else other_ref[...]).reshape(sources * sites, half)
        partial = lax.dot_general(rows, gains, (((0,), (0,)), ((), ())), preferred_element_type=jnp.float32)
        partial = partial.astype(out_ref.dtype)
        first = (core_ref[0] ^ turn) * (blocks // 2)
        for block in range(blocks // 2):
            for part in range(parts):
                out_ref[first + block, part] = partial[part * slab:(part + 1) * slab, block * share:(block + 1) * share]


def shifted(value, by, fill):
    count = value.shape[0]
    row = lax.broadcasted_iota(jnp.int32, value.shape, 0)
    moved = pltpu.roll(value, by % count, 0)
    inside = row >= by if by > 0 else row < count + by
    return jnp.where(inside, moved, fill)


def across(rate, states, sign):
    step = 1
    while step < ROWS:
        states = [s + rate * shifted(s, sign * step, 0.0) for s in states]
        rate = rate * shifted(rate, sign * step, 1.0)
        step *= 2
    return shifted(rate, sign, 1.0), [shifted(s, sign, 0.0) for s in states]


def scan_kernel(parts_ref, decay_ref, persist_ref, smooth_ref, entry_ref, product_ref, summary_ref, inj):
    sources, slab, width = parts_ref.shape
    total = parts_ref[0].astype(jnp.float32)
    for source in range(1, sources):
        total = total + parts_ref[source].astype(jnp.float32)
    inj[...] = jnp.sqrt(1.0 - decay_ref[...] * decay_ref[...]) * total
    depth = slab // ROWS
    persist = persist_ref[...]

    def rows(ref, j):
        return ref[pl.ds(j, ROWS, stride=depth), :]

    decays = [rows(decay_ref, j) for j in range(depth)]
    decayed, local = [decays[0]], [rows(inj, 0)]
    for j in range(1, depth):
        decayed.append(decays[j] * decayed[-1])
        local.append(decays[j] * local[-1] + rows(inj, j))
    enter_rate, (enter,) = across(decayed[-1], [local[-1]], 1)
    local = [h + a * enter for h, a in zip(local, decayed)]
    decayed = [a * enter_rate for a in decayed]
    products, smooth, entry = [None] * depth, [None] * depth, [None] * depth
    for j in reversed(range(depth)):
        rate = persist * decays[j]
        keep = 1.0 - rate * decays[j]
        if j == depth - 1:
            products[j], smooth[j], entry[j] = rate, keep * local[j], keep * decayed[j]
        else:
            products[j] = rate * products[j + 1]
            smooth[j] = rate * smooth[j + 1] + keep * local[j]
            entry[j] = rate * entry[j + 1] + keep * decayed[j]
    leave_rate, (leave_smooth, leave_entry) = across(products[0], [smooth[0], entry[0]], -1)
    for j in range(depth):
        smooth[j] = smooth[j] + products[j] * leave_smooth
        entry[j] = entry[j] + products[j] * leave_entry
        products[j] = products[j] * leave_rate
        smooth_ref[pl.ds(j, ROWS, stride=depth), :] = smooth[j]
        entry_ref[pl.ds(j, ROWS, stride=depth), :] = entry[j]
        product_ref[pl.ds(j, ROWS, stride=depth), :] = products[j]
    summary = [decayed[-1][ROWS - 1:], local[-1][ROWS - 1:], products[0][:1], smooth[0][:1], entry[0][:1]]
    summary = jnp.concatenate(summary + [jnp.zeros((3, width), jnp.float32)], axis=0)
    for to in range(summary_ref.shape[0]):
        summary_ref[to] = summary


def finish_kernel(place_ref, slabs_ref, smooth_ref, entry_ref, product_ref, rounded_ref, fwd, bwd):
    count, _, width = slabs_ref.shape

    def of(at, what):
        return slabs_ref[at, what:what + 1, :]

    state = jnp.zeros((1, width), jnp.float32)
    for at in range(count):
        fwd[at:at + 1, :] = state
        state = of(at, 0) * state + of(at, 1)
    state = jnp.zeros((1, width), jnp.float32)
    for at in reversed(range(count)):
        bwd[at:at + 1, :] = state
        state = of(at, 2) * state + (of(at, 3) + of(at, 4) * fwd[at:at + 1, :])
    place = place_ref[0]
    f_in, g_in = fwd[pl.ds(place, 1), :], bwd[pl.ds(place, 1), :]
    smoothed = smooth_ref[...] + entry_ref[...] * f_in + product_ref[...] * g_in
    rounded = smoothed.T.astype(rounded_ref.dtype)
    for to in range(rounded_ref.shape[0]):
        rounded_ref[to] = rounded


def predict_kernel(where_ref, near_ref, far_ref, mine_ref, pair_ref, out_ref):
    blocks, share, slab = mine_ref.shape
    pairs, _, sites, span = out_ref.shape
    first, core = where_ref[0] == 0, where_ref[1]
    mine, pair = mine_ref[...].reshape(blocks * share, slab), pair_ref[...].reshape(blocks * share, slab)
    states = jnp.concatenate([jnp.where(first, mine, pair), jnp.where(first, pair, mine)], axis=1)
    loadings = jnp.concatenate([near_ref[...], far_ref[...]], axis=0)
    predicted = jnp.dot(loadings, states, preferred_element_type=jnp.float32)
    predicted = predicted.astype(out_ref.dtype).reshape(2, pairs, sites, span)
    for other in range(2):
        out_ref[:, core ^ other] = predicted[other]


def call(kernel, name, out_shape, *args, scratch=(), scalars=0, vmem=32, **grid):
    if "in_specs" not in grid:
        specs = [pl.BlockSpec(memory_space=pltpu.SMEM)] * scalars
        specs += [pl.BlockSpec(memory_space=pltpu.VMEM)] * (len(args) - scalars)
        grid = dict(in_specs=specs)
    return pl.pallas_call(
        kernel,
        out_shape=out_shape,
        scratch_shapes=list(scratch),
        compiler_params=pltpu.CompilerParams(vmem_limit_bytes=vmem << 20),
        name=name,
        **grid,
    )(*args)


def per_device(observations, site_start, site_count, site_gain, site_loading, decay, persistence):
    planes, col, plane = ("zh", "zl"), ("y", "core"), ("x", "y", "core")
    line = plane + ("zl",)
    blocks, parts, nc = lax.axis_size("zh"), lax.axis_size("zl"), lax.axis_size(col)
    devices, slabs = lax.axis_size(plane), lax.axis_size(line)
    sites, epochs = observations.shape
    slab, span = epochs // slabs, epochs // devices
    basis = site_gain.shape[1]
    share = basis // blocks
    f32, bf16 = jnp.float32, jnp.bfloat16
    shape = jax.ShapeDtypeStruct
    turn = [
        ((h * parts + l) * nc + c, (c * parts + l) * nc + h)
        for h in range(blocks) for l in range(parts) for c in range(nc)
    ]

    hbm, smem = pl.BlockSpec(memory_space=pl.ANY), pltpu.SMEM
    sent = call(
        front_kernel, "front", shape((devices, sites, span + basis // 2), bf16),
        site_start, site_count, observations, site_gain, in_specs=[hbm] * 4, out_specs=hbm, vmem=60,
        scratch=[
            smem((sites,), jnp.int32), smem((sites,), jnp.int32),
            pltpu.VMEM((sites, epochs), bf16), pltpu.VMEM((sites, basis), bf16),
            pltpu.VMEM((devices, sites, span + basis // 2), bf16),
            pltpu.SemaphoreType.DMA((3,)), pltpu.SemaphoreType.DMA((STEPS,)), pltpu.SemaphoreType.DMA((STEPS,)),
        ],
    )
    got = lax.all_to_all(sent, plane, 0, 0, tiled=True)
    sources, sites, half = other_ref.shape
    blocks, parts, slab, share = out_ref.shape
    span = parts * slab
    rows = got_ref[:, :, :span].reshape(sources * sites, span)
    for turn in range(2):
        gains = (got_ref[:, :, span:] if turn == 0 else other_ref[...]).reshape(sources * sites, half)
        partial = lax.dot_general(rows, gains, (((0,), (0,)), ((), ())), preferred_element_type=jnp.float32)
        partial = partial.astype(out_ref.dtype)
        first = (core_ref[0] ^ turn) * (blocks // 2)
        for block in range(blocks // 2):
            for part in range(parts):
                out_ref[first + block, part] = partial[part * slab:(part + 1) * slab, block * share:(block + 1) * share]


def shifted(value, by, fill):
    count = value.shape[0]
    row = lax.broadcasted_iota(jnp.int32, value.shape, 0)
    moved = pltpu.roll(value, by % count, 0)
    inside = row >= by if by > 0 else row < count + by
    return jnp.where(inside, moved, fill)


def across(rate, states, sign):
    step = 1
    while step < ROWS:
        states = [s + rate * shifted(s, sign * step, 0.0) for s in states]
        rate = rate * shifted(rate, sign * step, 1.0)
        step *= 2
    return shifted(rate, sign, 1.0), [shifted(s, sign, 0.0) for s in states]


def scan_kernel(parts_ref, decay_ref, persist_ref, smooth_ref, entry_ref, product_ref, summary_ref, inj):
    sources, slab, width = parts_ref.shape
    total = parts_ref[0].astype(jnp.float32)
    for source in range(1, sources):
        total = total + parts_ref[source].astype(jnp.float32)
    inj[...] = jnp.sqrt(1.0 - decay_ref[...] * decay_ref[...]) * total
    depth = slab // ROWS
    persist = persist_ref[...]

    def rows(ref, j):
        return ref[pl.ds(j, ROWS, stride=depth), :]

    decays = [rows(decay_ref, j) for j in range(depth)]
    decayed, local = [decays[0]], [rows(inj, 0)]
    for j in range(1, depth):
        decayed.append(decays[j] * decayed[-1])
        local.append(decays[j] * local[-1] + rows(inj, j))
    enter_rate, (enter,) = across(decayed[-1], [local[-1]], 1)
    local = [h + a * enter for h, a in zip(local, decayed)]
    decayed = [a * enter_rate for a in decayed]
    products, smooth, entry = [None] * depth, [None] * depth, [None] * depth
    for j in reversed(range(depth)):
        rate = persist * decays[j]
        keep = 1.0 - rate * decays[j]
        if j == depth - 1:
            products[j], smooth[j], entry[j] = rate, keep * local[j], keep * decayed[j]
        else:
            products[j] = rate * products[j + 1]
            smooth[j] = rate * smooth[j + 1] + keep * local[j]
            entry[j] = rate * entry[j + 1] + keep * decayed[j]
    leave_rate, (leave_smooth, leave_entry) = across(products[0], [smooth[0], entry[0]], -1)
    for j in range(depth):
        smooth[j] = smooth[j] + products[j] * leave_smooth
        entry[j] = entry[j] + products[j] * leave_entry
        products[j] = products[j] * leave_rate
        smooth_ref[pl.ds(j, ROWS, stride=depth), :] = smooth[j]
        entry_ref[pl.ds(j, ROWS, stride=depth), :] = entry[j]
        product_ref[pl.ds(j, ROWS, stride=depth), :] = products[j]
    summary = [decayed[-1][ROWS - 1:], local[-1][ROWS - 1:], products[0][:1], smooth[0][:1], entry[0][:1]]
    summary = jnp.concatenate(summary + [jnp.zeros((3, width), jnp.float32)], axis=0)
    for to in range(summary_ref.shape[0]):
        summary_ref[to] = summary


def finish_kernel(place_ref, slabs_ref, smooth_ref, entry_ref, product_ref, rounded_ref, fwd, bwd):
    count, _, width = slabs_ref.shape

    def of(at, what):
        return slabs_ref[at, what:what + 1, :]

    state = jnp.zeros((1, width), jnp.float32)
    for at in range(count):
        fwd[at:at + 1, :] = state
        state = of(at, 0) * state + of(at, 1)
    state = jnp.zeros((1, width), jnp.float32)
    for at in reversed(range(count)):
        bwd[at:at + 1, :] = state
        state = of(at, 2) * state + (of(at, 3) + of(at, 4) * fwd[at:at + 1, :])
    place = place_ref[0]
    f_in, g_in = fwd[pl.ds(place, 1), :], bwd[pl.ds(place, 1), :]
    smoothed = smooth_ref[...] + entry_ref[...] * f_in + product_ref[...] * g_in
    rounded = smoothed.T.astype(rounded_ref.dtype)
    for to in range(rounded_ref.shape[0]):
        rounded_ref[to] = rounded


def predict_kernel(where_ref, near_ref, far_ref, mine_ref, pair_ref, out_ref):
    blocks, share, slab = mine_ref.shape
    pairs, _, sites, span = out_ref.shape
    first, core = where_ref[0] == 0, where_ref[1]
    mine, pair = mine_ref[...].reshape(blocks * share, slab), pair_ref[...].reshape(blocks * share, slab)
    states = jnp.concatenate([jnp.where(first, mine, pair), jnp.where(first, pair, mine)], axis=1)
    loadings = jnp.concatenate([near_ref[...], far_ref[...]], axis=0)
    predicted = jnp.dot(loadings, states, preferred_element_type=jnp.float32)
    predicted = predicted.astype(out_ref.dtype).reshape(2, pairs, sites, span)
    for other in range(2):
        out_ref[:, core ^ other] = predicted[other]


def call(kernel, name, out_shape, *args, scratch=(), scalars=0, vmem=32, **grid):
    if "in_specs" not in grid:
        specs = [pl.BlockSpec(memory_space=pltpu.SMEM)] * scalars
        specs += [pl.BlockSpec(memory_space=pltpu.VMEM)] * (len(args) - scalars)
        grid = dict(in_specs=specs)
    return pl.pallas_call(
        kernel,
        out_shape=out_shape,
        scratch_shapes=list(scratch),
        compiler_params=pltpu.CompilerParams(vmem_limit_bytes=vmem << 20),
        name=name,
        **grid,
    )(*args)


def per_device(observations, site_start, site_count, site_gain, site_loading, decay, persistence):
    planes, col, plane = ("zh", "zl"), ("y", "core"), ("x", "y", "core")
    line = plane + ("zl",)
    blocks, parts, nc = lax.axis_size("zh"), lax.axis_size("zl"), lax.axis_size(col)
    devices, slabs = lax.axis_size(plane), lax.axis_size(line)
    sites, epochs = observations.shape
    slab, span = epochs // slabs, epochs // devices
    basis = site_gain.shape[1]
    share = basis // blocks
    f32, bf16 = jnp.float32, jnp.bfloat16
    shape = jax.ShapeDtypeStruct
    turn = [
        ((h * parts + l) * nc + c, (c * parts + l) * nc + h)
        for h in range(blocks) for l in range(parts) for c in range(nc)
    ]

    hbm, smem = pl.BlockSpec(memory_space=pl.ANY), pltpu.SMEM
    sent = call(
        front_kernel, "front", shape((devices, sites, span + basis // 2), bf16),
        site_start, site_count, observations, site_gain, in_specs=[hbm] * 4, out_specs=hbm, vmem=60,
        scratch=[
            smem((sites,), jnp.int32), smem((sites,), jnp.int32),
            pltpu.VMEM((sites, epochs), bf16), pltpu.VMEM((sites, basis), bf16),
            pltpu.VMEM((devices, sites, span + basis // 2), bf16),
            pltpu.SemaphoreType.DMA((3,)), pltpu.SemaphoreType.DMA((STEPS,)), pltpu.SemaphoreType.DMA((STEPS,)),
        ],
    )
    got = lax.all_to_all(sent, plane, 0, 0, tiled=True)
    own = lax.dynamic_slice_in_dim(decay, lax.axis_index(col) * share, share, 1)
    decays = lax.ppermute(own, planes + col, turn)
    persist = lax.dynamic_slice_in_dim(persistence, lax.axis_index("zh") * share, share, 0)[None]
    got, decays, persist = lax.optimization_barrier((got, decays, persist))

    swap = [(0, 1), (1, 0)]
    other = lax.ppermute(got[:, :, span:], "core", swap)
    own = lax.dynamic_slice_in_dim(decay, lax.axis_index(col) * share, share, 1)
    decays = lax.ppermute(own, planes + col, turn)
    persist = lax.dynamic_slice_in_dim(persistence, lax.axis_index("zh") * share, share, 0)[None]
    other, decays, persist = lax.optimization_barrier((other, decays, persist))
    core = lax.axis_index("core").astype(jnp.int32)
    partial = call(drive_kernel, "drive", shape((blocks, parts, slab, share), bf16), core[None], got, other, scalars=1)
    summed = lax.all_to_all(partial.reshape(blocks * parts, slab, share), planes, 0, 0, tiled=True)
    near, _ = lax.optimization_barrier((site_loading, other))
    near = lax.all_gather(near, ("x", "y"), axis=0, tiled=True)
    summed, near = lax.optimization_barrier((summed, near))
    square = shape((slab, share), f32)
    smooth, entry, product, summary = call(
        scan_kernel, "scan", (square, square, square, shape((slabs, 8, share), f32)), summed, decays, persist,
        scratch=[pltpu.VMEM((slab, share), f32)],
    )
    summaries = lax.all_to_all(summary, line, 0, 0, tiled=True)
    far = lax.ppermute(near, "core", [(0, 1), (1, 0)])
    summaries, near, far = lax.optimization_barrier((summaries, near, far))
    rounded = call(
        finish_kernel, "finish", shape((blocks, share, slab), bf16),
        lax.axis_index(line).astype(jnp.int32)[None], summaries, smooth, entry, product,
        scratch=[pltpu.VMEM((slabs, share), f32)] * 2, scalars=1,
    )

    mine = lax.all_to_all(rounded, "zh", 0, 0, tiled=True)
    pair = lax.ppermute(mine, "zl", [(0, 1), (1, 0)])
    own = lax.all_to_all(mine, col, 0, 0, tiled=True)

    cores = lax.axis_size("core")
    where = jnp.stack([lax.axis_index("zl"), lax.axis_index("core")]).astype(jnp.int32)
    predicted = call(
        predict_kernel, "predict", shape((devices // cores, cores, sites, span), bf16),
        where, near, far, mine, pair, scalars=1,
    )
    predicted, own = lax.optimization_barrier((predicted, own))
    out = lax.dynamic_index_in_dim(own, lax.axis_index("zh"), 0, False).T.astype(f32)
    back = lax.all_to_all(predicted.reshape(devices, sites, span), plane, 0, 0, tiled=True)
    return (out, back.transpose(1, 0, 2).reshape(sites, epochs))


def solution(mesh):
    fine = Mesh(mesh.devices.reshape(4, 8, 2, 4, 2), ("x", "zh", "zl", "y", "core"))
    tm, col = ("x", "zh", "zl"), ("y", "core")
    every = tm + col
    return jax.shard_map(
        per_device,
        mesh=fine,
        in_specs=(P(every, None), P(every), P(every), P(every, None), P(every, None), P(tm, None), P()),
        out_specs=(P(tm, col), P(every, None)),
        check_vma=False,
    )
```

```python
import jax
import jax.numpy as jnp
from jax import lax
from jax.experimental import pallas as pl
from jax.experimental.pallas import tpu as pltpu
from jax.sharding import Mesh, PartitionSpec as P

ROWS = 8
STEPS = 4


def front_kernel(start_hbm, count_hbm, values_hbm, gain_hbm, out_hbm, start, count, values, gain, copies, out, small, large, sent, gains_sent):
    devices, sites, span = out.shape
    wide, each = values.shape[1] // STEPS, devices // STEPS
    arriving = [
        pltpu.make_async_copy(start_hbm, start, small.at[0]),
        pltpu.make_async_copy(count_hbm, count, small.at[1]),
        pltpu.make_async_copy(gain_hbm, gain, small.at[2]),
    ]
    chunks = []
    for step in range(STEPS):
        part = (slice(None), pl.ds(step * wide, wide))
        chunks.append(pltpu.make_async_copy(values_hbm.at[part], values.at[part], large.at[step]))
    for copy in arriving + chunks:
        copy.start()
    arriving.pop().wait()
    leaving = []
    for at in range(each):
        copies[at] = gain[...]
    for step in range(STEPS):
        part = (pl.ds(step * each, each), slice(None), pl.ds(span, gain.shape[1]))
        leaving.append(pltpu.make_async_copy(copies, out_hbm.at[part], gains_sent.at[step]))
        leaving[-1].start()
    for copy in arriving:
        copy.wait()
    site = lax.broadcasted_iota(jnp.int32, (sites, span), 0)
    first = end = jnp.zeros((sites, span), jnp.int32)
    for s in range(sites):
        first = jnp.where(site == s, start[s], first)
        end = jnp.where(site == s, start[s] + count[s], end)
    epoch = lax.broadcasted_iota(jnp.int32, (sites, span), 1)
    for step in range(STEPS):
        chunks[step].wait()
        for to in range(step * each, (step + 1) * each):
            own = values[:, to * span:(to + 1) * span].astype(jnp.float32)
            inside = (epoch + to * span >= first) & (epoch + to * span < end)
            out[to] = jnp.where(inside, own, 0.0).astype(out.dtype)
        part = pl.ds(step * each, each)
        leaving.append(pltpu.make_async_copy(out.at[part], out_hbm.at[part, slice(None), pl.ds(0, span)], sent.at[step]))
        leaving[-1].start()
    for copy in leaving:
        copy.wait()


def drive_kernel(got_ref, out_ref):
    sources, sites, width = got_ref.shape
    blocks, parts, slab, share = out_ref.shape
    span = parts * slab
    rows = got_ref[:, :, :span].reshape(sources * sites, span)
    gains = got_ref[:, :, span:].reshape(sources * sites, blocks * share)
    partial = lax.dot_general(rows, gains, (((0,), (0,)), ((), ())), preferred_element_type=jnp.float32)
    partial = partial.astype(out_ref.dtype)
    for block in range(blocks):
        for part in range(parts):
            out_ref[block, part] = partial[part * slab:(part + 1) * slab, block * share:(block + 1) * share]


def shifted(value, by, fill):
    count = value.shape[0]
    row = lax.broadcasted_iota(jnp.int32, value.shape, 0)
    moved = pltpu.roll(value, by % count, 0)
    inside = row >= by if by > 0 else row < count + by
    return jnp.where(inside, moved, fill)


def across(rate, states, sign):
    step = 1
    while step < ROWS:
        states = [s + rate * shifted(s, sign * step, 0.0) for s in states]
        rate = rate * shifted(rate, sign * step, 1.0)
        step *= 2
    return shifted(rate, sign, 1.0), [shifted(s, sign, 0.0) for s in states]


def scan_kernel(parts_ref, decay_ref, persist_ref, smooth_ref, entry_ref, product_ref, summary_ref, inj):
    sources, slab, width = parts_ref.shape
    total = parts_ref[0].astype(jnp.float32)
    for source in range(1, sources):
        total = total + parts_ref[source].astype(jnp.float32)
    inj[...] = jnp.sqrt(1.0 - decay_ref[...] * decay_ref[...]) * total
    depth = slab // ROWS
    persist = persist_ref[...]

    def rows(ref, j):
        return ref[pl.ds(j, ROWS, stride=depth), :]

    decays = [rows(decay_ref, j) for j in range(depth)]
    decayed, local = [decays[0]], [rows(inj, 0)]
    for j in range(1, depth):
        decayed.append(decays[j] * decayed[-1])
        local.append(decays[j] * local[-1] + rows(inj, j))
    enter_rate, (enter,) = across(decayed[-1], [local[-1]], 1)
    local = [h + a * enter for h, a in zip(local, decayed)]
    decayed = [a * enter_rate for a in decayed]
    products, smooth, entry = [None] * depth, [None] * depth, [None] * depth
    for j in reversed(range(depth)):
        rate = persist * decays[j]
        keep = 1.0 - rate * decays[j]
        if j == depth - 1:
            products[j], smooth[j], entry[j] = rate, keep * local[j], keep * decayed[j]
        else:
            products[j] = rate * products[j + 1]
            smooth[j] = rate * smooth[j + 1] + keep * local[j]
            entry[j] = rate * entry[j + 1] + keep * decayed[j]
    leave_rate, (leave_smooth, leave_entry) = across(products[0], [smooth[0], entry[0]], -1)
    for j in range(depth):
        smooth[j] = smooth[j] + products[j] * leave_smooth
        entry[j] = entry[j] + products[j] * leave_entry
        products[j] = products[j] * leave_rate
        smooth_ref[pl.ds(j, ROWS, stride=depth), :] = smooth[j]
        entry_ref[pl.ds(j, ROWS, stride=depth), :] = entry[j]
        product_ref[pl.ds(j, ROWS, stride=depth), :] = products[j]
    summary = [decayed[-1][ROWS - 1:], local[-1][ROWS - 1:], products[0][:1], smooth[0][:1], entry[0][:1]]
    summary = jnp.concatenate(summary + [jnp.zeros((3, width), jnp.float32)], axis=0)
    for to in range(summary_ref.shape[0]):
        summary_ref[to] = summary


def finish_kernel(place_ref, slabs_ref, smooth_ref, entry_ref, product_ref, rounded_ref, fwd, bwd):
    count, _, width = slabs_ref.shape

    def of(at, what):
        return slabs_ref[at, what:what + 1, :]

    state = jnp.zeros((1, width), jnp.float32)
    for at in range(count):
        fwd[at:at + 1, :] = state
        state = of(at, 0) * state + of(at, 1)
    state = jnp.zeros((1, width), jnp.float32)
    for at in reversed(range(count)):
        bwd[at:at + 1, :] = state
        state = of(at, 2) * state + (of(at, 3) + of(at, 4) * fwd[at:at + 1, :])
    place = place_ref[0]
    f_in, g_in = fwd[pl.ds(place, 1), :], bwd[pl.ds(place, 1), :]
    smoothed = smooth_ref[...] + entry_ref[...] * f_in + product_ref[...] * g_in
    rounded = smoothed.T.astype(rounded_ref.dtype)
    for to in range(rounded_ref.shape[0]):
        rounded_ref[to] = rounded


def predict_kernel(where_ref, near_ref, far_ref, mine_ref, pair_ref, out_ref):
    blocks, share, slab = mine_ref.shape
    pairs, _, sites, span = out_ref.shape
    first, core = where_ref[0] == 0, where_ref[1]
    mine, pair = mine_ref[...].reshape(blocks * share, slab), pair_ref[...].reshape(blocks * share, slab)
    states = jnp.concatenate([jnp.where(first, mine, pair), jnp.where(first, pair, mine)], axis=1)
    loadings = jnp.concatenate([near_ref[...], far_ref[...]], axis=0)
    predicted = jnp.dot(loadings, states, preferred_element_type=jnp.float32)
    predicted = predicted.astype(out_ref.dtype).reshape(2, pairs, sites, span)
    for other in range(2):
        out_ref[:, core ^ other] = predicted[other]


def call(kernel, name, out_shape, *args, scratch=(), scalars=0, vmem=32, **grid):
    if "in_specs" not in grid:
        specs = [pl.BlockSpec(memory_space=pltpu.SMEM)] * scalars
        specs += [pl.BlockSpec(memory_space=pltpu.VMEM)] * (len(args) - scalars)
        grid = dict(in_specs=specs)
    return pl.pallas_call(
        kernel,
        out_shape=out_shape,
        scratch_shapes=list(scratch),
        compiler_params=pltpu.CompilerParams(vmem_limit_bytes=vmem << 20),
        name=name,
        **grid,
    )(*args)


def per_device(observations, site_start, site_count, site_gain, site_loading, decay, persistence):
    planes, col, plane = ("zh", "zl"), ("y", "core"), ("x", "y", "core")
    line = plane + ("zl",)
    blocks, parts, nc = lax.axis_size("zh"), lax.axis_size("zl"), lax.axis_size(col)
    devices, slabs = lax.axis_size(plane), lax.axis_size(line)
    sites, epochs = observations.shape
    slab, span = epochs // slabs, epochs // devices
    basis = site_gain.shape[1]
    share = basis // blocks
    f32, bf16 = jnp.float32, jnp.bfloat16
    shape = jax.ShapeDtypeStruct
    turn = [
        ((h * parts + l) * nc + c, (c * parts + l) * nc + h)
        for h in range(blocks) for l in range(parts) for c in range(nc)
    ]

    hbm, smem = pl.BlockSpec(memory_space=pl.ANY), pltpu.SMEM
    sent = call(
        front_kernel, "front", shape((devices, sites, span + basis), bf16),
        site_start, site_count, observations, site_gain, in_specs=[hbm] * 4, out_specs=hbm, vmem=60,
        scratch=[
            smem((sites,), jnp.int32), smem((sites,), jnp.int32),
            pltpu.VMEM((sites, epochs), bf16), pltpu.VMEM((sites, basis), bf16),
            pltpu.VMEM((devices // STEPS, sites, basis), bf16), pltpu.VMEM((devices, sites, span), bf16),
            pltpu.SemaphoreType.DMA((3,)), pltpu.SemaphoreType.DMA((STEPS,)), pltpu.SemaphoreType.DMA((STEPS,)),
            pltpu.SemaphoreType.DMA((STEPS,)),
        ],
    )
    got = lax.all_to_all(sent, plane, 0, 0, tiled=True)
    own = lax.dynamic_slice_in_dim(decay, lax.axis_index(col) * share, share, 1)
    decays = lax.ppermute(own, planes + col, turn)
    persist = lax.dynamic_slice_in_dim(persistence, lax.axis_index("zh") * share, share, 0)[None]
    got, decays, persist = lax.optimization_barrier((got, decays, persist))

    partial = call(drive_kernel, "drive", shape((blocks, parts, slab, share), bf16), got)
    summed = lax.all_to_all(partial.reshape(blocks * parts, slab, share), planes, 0, 0, tiled=True)
    near, _ = lax.optimization_barrier((site_loading, got))
    near = lax.all_gather(near, ("x", "y"), axis=0, tiled=True)
    summed, near = lax.optimization_barrier((summed, near))
    square = shape((slab, share), f32)
    smooth, entry, product, summary = call(
        scan_kernel, "scan", (square, square, square, shape((slabs, 8, share), f32)), summed, decays, persist,
        scratch=[pltpu.VMEM((slab, share), f32)],
    )
    summaries = lax.all_to_all(summary, line, 0, 0, tiled=True)
    far = lax.ppermute(near, "core", [(0, 1), (1, 0)])
    summaries, near, far = lax.optimization_barrier((summaries, near, far))
    rounded = call(
        finish_kernel, "finish", shape((blocks, share, slab), bf16),
        lax.axis_index(line).astype(jnp.int32)[None], summaries, smooth, entry, product,
        scratch=[pltpu.VMEM((slabs, share), f32)] * 2, scalars=1,
    )

    mine = lax.all_to_all(rounded, "zh", 0, 0, tiled=True)
    pair = lax.ppermute(mine, "zl", [(0, 1), (1, 0)])
    own = lax.all_to_all(mine, col, 0, 0, tiled=True)

    cores = lax.axis_size("core")
    where = jnp.stack([lax.axis_index("zl"), lax.axis_index("core")]).astype(jnp.int32)
    predicted = call(
        predict_kernel, "predict", shape((devices // cores, cores, sites, span), bf16),
        where, near, far, mine, pair, scalars=1,
    )
    predicted, own = lax.optimization_barrier((predicted, own))
    out = lax.dynamic_index_in_dim(own, lax.axis_index("zh"), 0, False).T.astype(f32)
    back = lax.all_to_all(predicted.reshape(devices, sites, span), plane, 0, 0, tiled=True)
    return (out, back.transpose(1, 0, 2).reshape(sites, epochs))


def solution(mesh):
    fine = Mesh(mesh.devices.reshape(4, 8, 2, 4, 2), ("x", "zh", "zl", "y", "core"))
    tm, col = ("x", "zh", "zl"), ("y", "core")
    every = tm + col
    return jax.shard_map(
        per_device,
        mesh=fine,
        in_specs=(P(every, None), P(every), P(every), P(every, None), P(every, None), P(tm, None), P()),
        out_specs=(P(tm, col), P(every, None)),
        check_vma=False,
    )
```
